32 devices in a mesh: dp: 8 (over z, core), tensor: 4 (over y, x).
Axes of the slice: x: 2, y: 2, z: 4, core: 2. Of those that a mesh axis runs over, the one named last changes fastest.
Arguments:
- block_input: bfloat16 [8192, 2048], P(('dp', 'tensor')), may hold values from -6 to 6
- out_grad: bfloat16 [8192, 2048], P(('dp', 'tensor')), may hold values from -6 to 6
- routes: int32 [8192, 2], P('dp'), may hold values from 0 to 7, all different within a row
- prefixes: int32 [8], P('dp'), may hold values from 102 to 512
- drop_order: int32 [8, 1024], P('dp'), may hold values from 0 to 1023, each once within a row
- attn_gain: bfloat16 [2048], P(('dp', 'tensor')), may hold values from 0.5 to 1.5
- query_proj: bfloat16 [2048, 3072], P('dp', 'tensor'), may hold values from -0.125 to 0.125
- kv_down: bfloat16 [2048, 576], P(('dp', 'tensor')), may hold values from -0.125 to 0.125
- kv_gain: bfloat16 [512], P(('dp', 'tensor')), may hold values from 0.5 to 1.5
- kv_up: bfloat16 [512, 4096], P('dp', 'tensor'), may hold values from -0.25 to 0.25
- out_proj: bfloat16 [2048, 2048], P('tensor', 'dp'), may hold values from -1 to 1
- ffn_gain: bfloat16 [2048], P(('dp', 'tensor')), may hold values from 0.5 to 1.5
- router_proj: bfloat16 [2048, 8], P(('dp', 'tensor')), may hold values from -0.0625 to 0.0625
- shared_gate: bfloat16 [2048, 2816], P('dp', 'tensor'), may hold values from -0.125 to 0.125
- shared_up: bfloat16 [2048, 2816], P('dp', 'tensor'), may hold values from -0.125 to 0.125
- shared_down: bfloat16 [2816, 2048], P('tensor', 'dp'), may hold values from -0.15625 to 0.15625
- expert_gate: bfloat16 [8, 2048, 1408], P(None, 'dp', 'tensor'), may hold values from -0.125 to 0.125
- expert_up: bfloat16 [8, 2048, 1408], P(None, 'dp', 'tensor'), may hold values from -0.125 to 0.125
- expert_down: bfloat16 [8, 1408, 2048], P(None, 'tensor', 'dp'), may hold values from -1.25 to 1.25
Outputs:
- output: bfloat16 [8192, 2048], P(('dp', 'tensor'))
- input_grad: float32 [8192, 2048], P(('dp', 'tensor'))
- grad_attn_gain: float32 [2048], P(('dp', 'tensor'))
- grad_query_proj: float32 [2048, 3072], P('dp', 'tensor')
- grad_kv_down: float32 [2048, 576], P(('dp', 'tensor'))
- grad_kv_gain: float32 [512], P(('dp', 'tensor'))
- grad_kv_up: float32 [512, 4096], P('dp', 'tensor')
- grad_out_proj: float32 [2048, 2048], P('tensor', 'dp')
- grad_ffn_gain: float32 [2048], P(('dp', 'tensor'))
- grad_router_proj: float32 [2048, 8], P(('dp', 'tensor'))
- grad_shared_gate: float32 [2048, 2816], P('dp', 'tensor')
- grad_shared_up: float32 [2048, 2816], P('dp', 'tensor')
- grad_shared_down: float32 [2816, 2048], P('tensor', 'dp')
- grad_expert_gate: float32 [8, 2048, 1408], P(None, 'dp', 'tensor')
- grad_expert_up: float32 [8, 2048, 1408], P(None, 'dp', 'tensor')
- grad_expert_down: float32 [8, 1408, 2048], P(None, 'tensor', 'dp')
The draws below stay inside these ranges and needn't reach their ends.
Inputs may be any that keep to these rules, and one draw needn't show every extreme that they name: `routes`: each token names 2 different experts; every expert is named by some token. `drop_order`: each row names every token place of its group once.
All inputs are finite; a program needn't handle non-finite values.
Results may differ from the reference program's by a relative error of at most 0.024.
Values may be sent and summed in bfloat16 or wider, within the bound.
No kernel may reach another device: no remote copies, remote signals or barrier semaphores. Data moves between devices by JAX's collectives and lax.ppermute only.
A program may use at most 384 MiB of HBM per device.

```python
import jax
import jax.numpy as jnp
from jax import lax

D = 2048
HEADS = 16
NOPE = 128
ROPE = 64
VD = 128
KVR = 512
F = 1408
SF = 2816
TOP = 2
EXPERTS = 8
LENGTH = 1024
GROUP_TOK = 1024
GROUPS = 8
SEQS = 8
TOKENS = 8192
CAP = 288


def set_ends(values, key, low, largest):
    longest = values.shape.index(max(values.shape))
    spots = []
    for shift in (0, 1):
        where = [jax.random.randint(jax.random.fold_in(key, axis), (), 0, length) for axis, length in enumerate(values.shape)]
        where[longest] = (where[longest] + shift) % values.shape[longest]
        spots.append(tuple(where))
    return values.at[spots[0]].set(low).at[spots[1]].set(largest)


def block_levels(rng, extent, cuts, smallest, top_value):
    factor_of = 1.0
    for axis_at, parts in cuts:
        heights = jax.random.uniform(jax.random.fold_in(jax.random.fold_in(rng, 6), axis_at), (parts,), jnp.float32, smallest / len(cuts), top_value / len(cuts))
        factor_of = factor_of * jnp.repeat(jnp.exp(heights), extent[axis_at] // parts).reshape((-1,) + (1,) * (len(extent) - 1 - axis_at))
    return factor_of


def picks_of(own_key, rows, amount, top, lift):
    order = jax.random.permutation(jax.random.fold_in(own_key, 1), amount)
    favour = order
    for power in range(3):
        favour = favour * favour // amount
    favour = favour * lift // amount
    lots = jax.random.randint(jax.random.fold_in(own_key, 2), (rows, amount), 0, 4096) + favour
    holders = jax.random.permutation(jax.random.fold_in(own_key, 3), rows)[jnp.arange(amount) % rows]
    lots = jnp.where(jnp.arange(rows)[:, None] == holders[None, :], 1 << 14, lots)
    priority = lots * amount + jnp.arange(amount)
    return lax.top_k(priority.astype(jnp.int32), top)[1].astype(jnp.int32)


def centred(rng, shape, scale, reach, cuts=(), held_as=jnp.bfloat16):
    array = jax.random.normal(rng, shape, jnp.float32) * scale
    if len(cuts) > 0:
        array = block_levels(rng, shape, cuts, -0.22, 0.18) * array
    return jnp.clip(array, min=-reach, max=reach).astype(held_as)


def setup_inputs(seed: int = 0) -> dict:
    keys = jax.random.split(jax.random.key(seed), 20)
    block_input = centred(keys[0], (TOKENS, D), 1.0, 6.0, ((0, 32),))
    out_grad = centred(keys[1], (TOKENS, D), 1.0, 6.0, ((0, 32),))
    routes = picks_of(keys[2], TOKENS, EXPERTS, TOP, 2048)
    prefixes = set_ends(jax.random.randint(keys[3], (SEQS,), LENGTH // 10, LENGTH // 2 + 1), jax.random.fold_in(keys[3], 1), LENGTH // 10, (LENGTH // 2 + 1) - 1).astype(jnp.int32)
    drop_order = jax.vmap(lambda own: jax.random.permutation(own, GROUP_TOK))(jax.random.split(keys[4], GROUPS)).reshape((GROUPS, GROUP_TOK)).astype(jnp.int32)
    attn_gain = jnp.clip(1.0 + 0.1 * jax.random.normal(keys[5], (D,), jnp.float32), 0.5, 1.5).astype(jnp.bfloat16)
    query_proj = centred(keys[6], (D, HEADS * (NOPE + ROPE)), D ** -0.5, 0.125, ((0, 8), (1, 4)))
    kv_down = centred(keys[7], (D, KVR + ROPE), D ** -0.5, 0.125, ((0, 32),))
    kv_gain = jnp.clip(1.0 + 0.1 * jax.random.normal(keys[8], (KVR,), jnp.float32), 0.5, 1.5).astype(jnp.bfloat16)
    kv_up = centred(keys[9], (KVR, HEADS * (NOPE + VD)), KVR ** -0.5, 0.25, ((0, 8), (1, 4)))
    out_proj = centred(keys[10], (HEADS * VD, D), (HEADS * VD // 64) ** -0.5, 1.0, ((0, 4), (1, 8)))
    ffn_gain = jnp.clip(1.0 + 0.1 * jax.random.normal(keys[11], (D,), jnp.float32), 0.5, 1.5).astype(jnp.bfloat16)
    router_proj = centred(keys[12], (D, EXPERTS), (4 * D) ** -0.5, 0.0625, ((0, 32),))
    shared_gate = centred(keys[13], (D, SF), D ** -0.5, 0.125, ((0, 8), (1, 4)))
    shared_up = centred(keys[14], (D, SF), D ** -0.5, 0.125, ((0, 8), (1, 4)))
    shared_down = centred(keys[15], (SF, D), (SF // 2) ** -0.5, 0.15625, ((0, 4), (1, 8)))
    expert_gate = centred(keys[16], (EXPERTS, D, F), D ** -0.5, 0.125, ((1, 8), (2, 4)))
    expert_up = centred(keys[17], (EXPERTS, D, F), D ** -0.5, 0.125, ((1, 8), (2, 4)))
    expert_down = centred(keys[18], (EXPERTS, F, D), (F // 64) ** -0.5, 1.25, ((1, 4), (2, 8)))
    return {"block_input": block_input, "out_grad": out_grad, "routes": routes, "prefixes": prefixes, "drop_order": drop_order, "attn_gain": attn_gain, "query_proj": query_proj, "kv_down": kv_down, "kv_gain": kv_gain, "kv_up": kv_up, "out_proj": out_proj, "ffn_gain": ffn_gain, "router_proj": router_proj, "shared_gate": shared_gate, "shared_up": shared_up, "shared_down": shared_down, "expert_gate": expert_gate, "expert_up": expert_up, "expert_down": expert_down}


eps = 1e-06

@jax.custom_vjp
def low(v):
    return lax.optimization_barrier(v.astype(jnp.bfloat16)).astype(jnp.float32)

@jax.custom_vjp
def low_back(v):
    return v

def low_keep(v):
    return (low(v), None)

def low_pass(kept, grad):
    return (grad,)

def back_keep(v):
    return (v, None)

def back_low(kept, grad):
    return (low(grad),)
low.defvjp(low_keep, low_pass)
low_back.defvjp(back_keep, back_low)

def matmul_high(left, right):
    return jnp.dot(left, right, preferred_element_type=jnp.float32, precision=lax.Precision.HIGHEST)

def norm_rows(values, gain_vec):
    return values * lax.rsqrt(lax.optimization_barrier(jnp.mean(values * values, axis=-1, keepdims=True)) + eps) * gain_vec

def rotary_tables(row_count):
    half_width = ROPE // 2
    places = (jnp.arange(row_count, dtype=jnp.int32) % LENGTH).astype(jnp.float32)
    frequency = jnp.exp(-jnp.log(10000.0) * jnp.arange(half_width, dtype=jnp.int32).astype(jnp.float32) / half_width)
    angles = places[:, None] * frequency[None, :]
    return (jnp.cos(angles), jnp.sin(angles))

def rotate(values, cosine, sine_table):
    half_width = values.shape[-1] // 2
    front = values[..., :half_width]
    behind = values[..., half_width:]
    return jnp.concatenate([front * cosine - behind * sine_table, behind * cosine + front * sine_table], axis=-1)

def route_slots(routes, line_order, expert_table, capacity):
    row_count = routes.shape[0]
    token_ids = jnp.arange(row_count, dtype=jnp.int32)
    ranking = jnp.zeros((row_count,), jnp.int32).at[line_order].set(token_ids)
    chosen = lax.optimization_barrier(jnp.sum((routes[:, :, None] == jnp.arange(expert_table, dtype=jnp.int32)[None, None, :]).astype(jnp.int32), axis=1))
    in_line = chosen[line_order]
    before = jnp.cumsum(in_line, axis=0) - in_line
    slot_rank = jnp.take_along_axis(before[ranking], routes, axis=1)
    kept_mask = slot_rank < capacity
    flat_slot = jnp.where(kept_mask, routes * capacity + slot_rank, expert_table * capacity).astype(jnp.int32)
    slot_token = jnp.full((expert_table * capacity + 1,), row_count, jnp.int32).at[flat_slot.reshape(-1)].set(jnp.repeat(token_ids, routes.shape[1]))
    return (kept_mask, flat_slot, slot_token[:expert_table * capacity].reshape(expert_table, capacity))

def attend_one(pieces):
    seq_query, seq_nope, seq_rope, seq_values, prefix = pieces
    positions = jnp.arange(LENGTH, dtype=jnp.int32)
    allowed = (positions[None, :] <= positions[:, None]) | (positions[None, :] < prefix)
    key_full = jnp.concatenate([seq_nope, jnp.broadcast_to(seq_rope[:, None, :], (LENGTH, seq_nope.shape[1], ROPE))], axis=-1)
    scores = low_back(jnp.einsum('qhc,khc->hqk', seq_query, key_full, precision=lax.Precision.HIGHEST))
    scores = jnp.where(allowed[None], scores, -1e+30)
    attn_probs = jax.nn.softmax(scores, axis=-1)
    return jnp.einsum('hqk,khv->qhv', low(attn_probs), seq_values, precision=lax.Precision.HIGHEST)

def block_forward(xin, weights, prefix_part, route_part, order_part):
    attn_gain, query_proj, kv_down, kv_gain, kv_up, out_proj, ffn_gain, router_proj, shared_gate, shared_up, shared_down, expert_gate, expert_up, expert_down = weights
    group_rows = xin.shape[0]
    qk_width = NOPE + ROPE
    cosine, sine_table = rotary_tables(group_rows)
    normed_one = low(norm_rows(xin, attn_gain))
    query_raw = low_back(matmul_high(normed_one, query_proj)).reshape(group_rows, HEADS, qk_width)
    queries = low(jnp.concatenate([query_raw[..., :NOPE], rotate(query_raw[..., NOPE:], cosine[:, None, :], sine_table[:, None, :])], axis=-1) * qk_width ** (-0.5))
    compressed = low_back(matmul_high(normed_one, kv_down))
    latent = low(norm_rows(compressed[:, :KVR], kv_gain))
    key_rope = low(rotate(compressed[:, KVR:], cosine, sine_table))
    key_value = low(low_back(matmul_high(latent, kv_up))).reshape(group_rows, HEADS, NOPE + VD)
    seq_count = group_rows // LENGTH
    attended = lax.map(jax.checkpoint(attend_one), (queries.reshape(seq_count, LENGTH, HEADS, qk_width), key_value[..., :NOPE].reshape(seq_count, LENGTH, HEADS, NOPE), key_rope.reshape(seq_count, LENGTH, ROPE), key_value[..., NOPE:].reshape(seq_count, LENGTH, HEADS, VD), prefix_part))
    attended = low(low_back(attended.reshape(group_rows, HEADS * VD)))
    middle = xin + low_back(matmul_high(attended, out_proj))
    normed_two = low(norm_rows(middle, ffn_gain))
    router = jax.nn.softmax(low_back(matmul_high(normed_two, router_proj)), axis=-1)
    kept_mask, flat_slot, slot_token = route_slots(route_part, order_part, EXPERTS, CAP)
    route_gates = jnp.take_along_axis(router, route_part, axis=1) * kept_mask.astype(jnp.float32)
    padded_in = jnp.concatenate([normed_two, jnp.zeros((1, D), jnp.float32)], axis=0)
    inputs = padded_in[slot_token]
    gate_val = low_back(jnp.einsum('ecd,edf->ecf', inputs, expert_gate, precision=lax.Precision.HIGHEST))
    up_val = low_back(jnp.einsum('ecd,edf->ecf', inputs, expert_up, precision=lax.Precision.HIGHEST))
    hidden = low(jax.nn.silu(gate_val) * up_val)
    outputs = low_back(jnp.einsum('ecf,efd->ecd', hidden, expert_down, precision=lax.Precision.HIGHEST))
    flat_out = jnp.concatenate([outputs.reshape(EXPERTS * CAP, D), jnp.zeros((1, D), jnp.float32)], axis=0)
    routed = jnp.einsum('tk,tkd->td', route_gates, flat_out[flat_slot], precision=lax.Precision.HIGHEST)
    shared_gate_val = low_back(matmul_high(normed_two, shared_gate))
    shared_up_val = low_back(matmul_high(normed_two, shared_up))
    shared_hidden = low(jax.nn.silu(shared_gate_val) * shared_up_val)
    return middle + routed + matmul_high(shared_hidden, shared_down)

def reference(block_input, out_grad, routes, prefixes, drop_order, attn_gain, query_proj, kv_down, kv_gain, kv_up, out_proj, ffn_gain, router_proj, shared_gate, shared_up, shared_down, expert_gate, expert_up, expert_down):
    weights = tuple((weight.astype(jnp.float32) for weight in (attn_gain, query_proj, kv_down, kv_gain, kv_up, out_proj, ffn_gain, router_proj, shared_gate, shared_up, shared_down, expert_gate, expert_up, expert_down)))
    group_count = drop_order.shape[0]
    group_rows = drop_order.shape[1]

    def one_group(totals, group_item):
        x_part, grad_part, route_part, prefix_part, order_part = group_item

        def forward(x_value, *weight_values):
            return block_forward(x_value, weight_values, prefix_part, route_part, order_part)
        result, pull = jax.vjp(forward, x_part.astype(jnp.float32), *weights)
        grads = pull(grad_part.astype(jnp.float32))
        totals = tuple((previous_value + new_value for previous_value, new_value in zip(totals, grads[1:])))
        return (totals, (result.astype(jnp.bfloat16), grads[0]))
    start_totals = tuple((jnp.zeros(weight.shape, jnp.float32) for weight in weights))
    totals, (results, input_grads) = lax.scan(one_group, start_totals, (block_input.reshape(group_count, group_rows, D), out_grad.reshape(group_count, group_rows, D), routes.reshape(group_count, group_rows, TOP), prefixes.reshape(group_count, group_rows // LENGTH), drop_order))
    return (results.reshape(group_count * group_rows, D), input_grads.reshape(group_count * group_rows, D), totals[0], totals[1], totals[2], totals[3], totals[4], totals[5], totals[6], totals[7], totals[8], totals[9], totals[10], totals[11], totals[12], totals[13])
```

```python
import jax
import jax.numpy as jnp
from jax import lax
from jax.sharding import PartitionSpec as P

D = 2048
NOPE = 128
ROPE = 64
VD = 128
KVR = 512
TOP = 2
LENGTH = 1024

eps = 1e-06
bf16 = jnp.bfloat16
f32 = jnp.float32


def dot(a, b, dims=((1,), (0,)), out=f32):
    return lax.dot_general(a, b, (dims, ((), ())), preferred_element_type=f32).astype(out)


def dot_nt(a, b, out=f32):
    return dot(a, b, ((1,), (1,)), out)


def dot_tn(a, b, out=f32):
    return dot(a, b, ((0,), (0,)), out)


def inv_rms(values):
    return lax.rsqrt(jnp.mean(values * values, axis=-1, keepdims=True) + eps)


def norm_rows(values, gain_vec):
    return values * inv_rms(values) * gain_vec


def norm_back(values, gain_vec, upstream):
    inv = inv_rms(values)
    scaled = upstream * gain_vec
    grad = inv * scaled - values * (
        inv * inv * inv * jnp.mean(values * scaled, axis=-1, keepdims=True)
    )
    return grad, jnp.sum(upstream * values * inv, axis=0)


def rotate(values, cosine, sine_table):
    half_width = values.shape[-1] // 2
    front = values[..., :half_width]
    behind = values[..., half_width:]
    return jnp.concatenate(
        [front * cosine - behind * sine_table, behind * cosine + front * sine_table], axis=-1
    )


def silu_back(gate_val, up_val, upstream):
    sigmoid_val = jax.nn.sigmoid(gate_val)
    return (
        upstream * up_val * sigmoid_val * (1.0 + gate_val * (1.0 - sigmoid_val)),
        upstream * gate_val * sigmoid_val,
    )


def swap_core(values):
    count = lax.axis_size("dp")
    return lax.ppermute(values, "dp", [(i, i ^ 1) for i in range(count)])


def gather_rows(values):
    count = lax.axis_size("tensor")
    return [values] + [
        lax.ppermute(values, "tensor", [(i, i ^ k) for i in range(count)])
        for k in range(count - 1, 0, -1)
    ][::-1]


def sum_rows(blocks):
    count = lax.axis_size("tensor")
    total = blocks[0].astype(f32)
    arrived = [
        lax.ppermute(blocks[k].astype(bf16), "tensor", [(i, i ^ k) for i in range(count)])
        for k in range(count - 1, 0, -1)
    ]
    for piece in arrived:
        total = total + piece.astype(f32)
    return total


def chain_reduce(blocks):
    count = lax.axis_size("dp")
    nz = count // 2
    place = lax.axis_index("dp") // 2
    rising = falling = None
    for step in range(nz - 1):
        up = lax.dynamic_index_in_dim(blocks, jnp.clip(nz - 1 - step + place, 0, nz - 1), 0, False)
        down = lax.dynamic_index_in_dim(blocks, jnp.clip(step - nz + 1 + place, 0, nz - 1), 0, False)
        if step > 0:
            up = (up.astype(f32) + rising.astype(f32)).astype(bf16)
            down = (down.astype(f32) + falling.astype(f32)).astype(bf16)
        rising = lax.ppermute(
            up,
            "dp",
            [(2 * j + c, 2 * j + 2 + c) for j in range(nz - 1) if j <= step for c in range(2)],
        )
        falling = lax.ppermute(
            down,
            "dp",
            [(2 * j + c, 2 * j - 2 + c) for j in range(1, nz) if nz - 1 - j <= step for c in range(2)],
        )
    mine = lax.dynamic_index_in_dim(blocks, place, 0, False).astype(f32)
    return mine + rising.astype(f32) + falling.astype(f32)


def reduce_dp(grad):
    count = lax.axis_size("dp")
    nz = count // 2
    rows = grad.shape[0] // count
    core = lax.axis_index("dp") % 2
    parts = grad.reshape(nz, 2, rows, grad.shape[1])
    other = lax.dynamic_index_in_dim(parts, 1 - core, 1, False)
    mine = lax.dynamic_index_in_dim(parts, core, 1, False)
    pair = (mine.astype(f32) + swap_core(other).astype(f32)).astype(bf16)
    return chain_reduce(pair)


def gather_dp(values):
    return lax.all_gather(values, "dp", axis=0, tiled=True)


def gather_z(values):
    count = lax.axis_size("dp")
    groups = [[2 * j + c for j in range(count // 2)] for c in range(2)]
    return lax.all_gather(values, "dp", axis=0, tiled=True, axis_index_groups=groups)


def attend_scores(queries, key_nope, key_rope, allowed):
    scores = jnp.einsum("qhc,khc->hqk", queries[..., :NOPE], key_nope, preferred_element_type=f32)
    scores = scores + jnp.einsum(
        "qhr,kr->hqk", queries[..., NOPE:], key_rope, preferred_element_type=f32
    )
    return jnp.where(allowed[None], scores, -1e30)


def attend_forward(queries, key_nope, key_rope, values_all, allowed):
    scores = attend_scores(queries, key_nope, key_rope, allowed)
    log_total = jax.nn.logsumexp(scores, axis=-1)
    weights = jnp.exp(scores - log_total[..., None]).astype(bf16)
    result = jnp.einsum("hqk,khv->qhv", weights, values_all, preferred_element_type=f32)
    return result, log_total


def attend_backward(queries, key_nope, key_rope, values_all, log_total, out_grad, allowed):
    scores = attend_scores(queries, key_nope, key_rope, allowed)
    weights = jnp.exp(scores - log_total[..., None])
    weight_grad = jnp.einsum("qhv,khv->hqk", out_grad, values_all, preferred_element_type=f32)
    inner = jnp.sum(weights * weight_grad, axis=-1, keepdims=True)
    score_grad = (weights * (weight_grad - inner)).astype(bf16)
    query_grad = jnp.concatenate(
        [
            jnp.einsum("hqk,khc->qhc", score_grad, key_nope, preferred_element_type=f32),
            jnp.einsum("hqk,kr->qhr", score_grad, key_rope, preferred_element_type=f32),
        ],
        axis=-1,
    )
    nope_grad = jnp.einsum(
        "hqk,qhc->khc", score_grad, queries[..., :NOPE], preferred_element_type=f32
    )
    rope_grad = jnp.einsum(
        "hqk,qhr->kr", score_grad, queries[..., NOPE:], preferred_element_type=f32
    )
    value_grad = jnp.einsum(
        "hqk,qhv->khv", weights.astype(bf16), out_grad, preferred_element_type=f32
    )
    return query_grad, nope_grad, rope_grad, value_grad


def on_device(
    block_input,
    out_grad,
    routes,
    prefixes,
    drop_order,
    attn_gain,
    query_proj,
    kv_down,
    kv_gain,
    kv_up,
    out_proj,
    ffn_gain,
    router_proj,
    shared_gate,
    shared_up,
    shared_down,
    expert_gate,
    expert_up,
    expert_down,
):
    me = lax.axis_index("tensor")
    place = lax.axis_index("dp")
    core = place % 2
    peers = lax.axis_size("tensor")
    dp_count = lax.axis_size("dp")
    nz = dp_count // 2
    local_rows = block_input.shape[0]
    rows = routes.shape[0]
    experts = expert_gate.shape[0]
    half = experts // 2
    capacity = rows * TOP * 9 // (8 * experts)
    qk_width = NOPE + ROPE
    query_scale = qk_width ** (-0.5)
    q_cols = query_proj.shape[1]
    heads = q_cols // qk_width
    d_rows = query_proj.shape[0]
    s_cols = shared_gate.shape[1]
    e_cols = expert_gate.shape[2]

    def in_order(array):
        return jnp.concatenate(
            [
                lax.dynamic_slice_in_dim(array, (me ^ k) * local_rows, local_rows, 0)
                for k in range(peers)
            ],
            axis=0,
        )

    x_all = jnp.concatenate(gather_rows(block_input), axis=0)
    go_all = jnp.concatenate(gather_rows(out_grad), axis=0)

    small_rows = kv_down.shape[0]

    def column(vector):
        return jnp.pad(vector, (0, small_rows - vector.shape[0]))[:, None]

    small = jnp.concatenate(
        [kv_down, router_proj, column(attn_gain), column(ffn_gain), column(kv_gain)], axis=1
    )
    small = jnp.pad(small, ((0, 0), (0, -small.shape[1] % 128)))
    small_blocks = gather_rows(small)
    small_all = jnp.zeros((peers * small_rows, small.shape[1]), bf16)
    for k, block in enumerate(small_blocks):
        small_all = lax.dynamic_update_slice_in_dim(small_all, block, (me ^ k) * small_rows, 0)
    front = gather_dp(jnp.concatenate([query_proj, small_all], axis=1))
    kv_cols = kv_down.shape[1]
    front_cols = q_cols + kv_cols
    query_full = front[:, :q_cols]
    down_full = front[:, q_cols:front_cols]
    router_full = front[:, front_cols : front_cols + experts]
    gain_at = front_cols + experts
    gain_one = front[:, gain_at].astype(f32)
    gain_two = front[:, gain_at + 1].astype(f32)
    gain_latent = (
        front[:, gain_at + 2].reshape(-1, small_rows)[:, : kv_gain.shape[0]].reshape(-1).astype(f32)
    )
    latent_up = gather_dp(kv_up)
    out_full = gather_dp(out_proj.T)
    shared_full = gather_dp(jnp.concatenate([shared_gate, shared_up, shared_down.T], axis=1))

    expert_local = jnp.concatenate(
        [expert_gate, expert_up, jnp.swapaxes(expert_down, 1, 2)], axis=2
    )
    kept_part = lax.dynamic_slice_in_dim(expert_local, core * half, half, 0)
    sent_part = lax.dynamic_slice_in_dim(expert_local, (1 - core) * half, half, 0)
    got_part = swap_core(sent_part)
    first = core == 0
    pair_part = jnp.concatenate(
        [jnp.where(first, kept_part, got_part), jnp.where(first, got_part, kept_part)], axis=1
    )
    expert_full = [gather_z(pair_part[s]) for s in range(half)]

    token_ids = jnp.arange(rows, dtype=jnp.int32)
    ranking = jnp.sum(
        jnp.where(drop_order[0][:, None] == token_ids[None, :], token_ids[:, None], 0), axis=0
    )
    expert_ids = jnp.arange(experts, dtype=jnp.int32)
    chosen = jnp.sum((routes[:, :, None] == expert_ids).astype(f32), axis=1)
    earlier = (ranking[None, :] < ranking[:, None]).astype(bf16)
    before = dot(earlier, chosen.astype(bf16)).astype(jnp.int32)
    slot_rank = jnp.sum(
        jnp.where(routes[:, :, None] == expert_ids, before[:, None, :], 0), axis=2
    )
    kept_mask = slot_rank < capacity
    flat_slot = in_order(jnp.where(kept_mask, routes * capacity + slot_rank, -1))
    routes_mine = in_order(routes)
    kept_mine = (flat_slot >= 0).astype(f32)
    slots = half * capacity
    slot_ids = jnp.arange(slots, dtype=jnp.int32)
    own_ids = core * slots + slot_ids
    far_ids = (1 - core) * slots + slot_ids

    def one_hot(ids):
        return (
            (flat_slot[:, 0:1] == ids[None, :]) | (flat_slot[:, 1:2] == ids[None, :])
        ).astype(bf16)

    own_hot = one_hot(own_ids)
    far_hot = one_hot(far_ids)

    def dispatch(values):
        return (
            dot_tn(own_hot, values, bf16).reshape(half, capacity, D),
            swap_core(dot_tn(far_hot, values, bf16)).reshape(half, capacity, D),
        )

    go_own, go_far = dispatch(go_all)

    places = in_order(token_ids).astype(f32)
    half_width = ROPE // 2
    frequency = jnp.exp(
        -jnp.log(10000.0) * jnp.arange(half_width, dtype=jnp.int32).astype(f32) / half_width
    )
    angles = places[:, None] * frequency[None, :]
    cosine, sine_table = jnp.cos(angles), jnp.sin(angles)
    places_int = in_order(token_ids)
    allowed = (places_int[None, :] <= places_int[:, None]) | (places_int[None, :] < prefixes[0])

    normed_all = norm_rows(x_all.astype(f32), gain_one).astype(bf16)
    query_raw = dot(normed_all, query_full).reshape(rows, heads, qk_width)
    queries = (
        jnp.concatenate(
            [
                query_raw[..., :NOPE],
                rotate(query_raw[..., NOPE:], cosine[:, None, :], sine_table[:, None, :]),
            ],
            axis=-1,
        )
        * query_scale
    ).astype(bf16)
    compressed = dot(normed_all, down_full)
    latent = norm_rows(compressed[:, :KVR], gain_latent).astype(bf16)
    key_rope = rotate(compressed[:, KVR:], cosine, sine_table).astype(bf16)
    key_value = dot(latent, latent_up, out=bf16).reshape(rows, heads, NOPE + VD)
    key_nope = key_value[..., :NOPE]
    values_all = key_value[..., NOPE:]
    attended, log_total = attend_forward(queries, key_nope, key_rope, values_all, allowed)
    attended = attended.astype(bf16).reshape(rows, heads * VD)

    def blocks_of(array):
        return [array[k * local_rows : (k + 1) * local_rows] for k in range(peers)]

    x_here = block_input.astype(f32)
    middle = x_here + sum_rows(blocks_of(dot_nt(attended, out_full)))
    normed_two = norm_rows(middle, gain_two).astype(bf16)
    h2 = jnp.concatenate(gather_rows(normed_two), axis=0)

    router = jax.nn.softmax(dot(h2, router_full), axis=-1)
    route_gates = jnp.sum(
        jnp.where(routes_mine[:, :, None] == expert_ids, router[:, None, :], 0.0), axis=2
    )

    def slot_gates(ids):
        return jnp.sum(
            jnp.where(flat_slot[:, 0:1] == ids[None, :], route_gates[:, 0:1], 0.0)
            + jnp.where(flat_slot[:, 1:2] == ids[None, :], route_gates[:, 1:2], 0.0),
            axis=0,
        )

    gate_own = slot_gates(own_ids).reshape(half, capacity)
    gate_far = swap_core(slot_gates(far_ids).reshape(half, capacity))

    shared_gu = shared_full[:, : 2 * s_cols]
    shared_dn = shared_full[:, 2 * s_cols :]
    shared_hidden_grad = dot(go_all, shared_dn)
    shared_val = dot(h2, shared_gu)
    sg, su = shared_val[:, :s_cols], shared_val[:, s_cols:]
    shared_hidden = (jax.nn.silu(sg) * su).astype(bf16)
    shared_back = jnp.concatenate(silu_back(sg, su, shared_hidden_grad), axis=1).astype(bf16)
    grad_shared = jnp.concatenate(
        [dot_tn(h2, shared_back, bf16), dot_tn(go_all, shared_hidden, bf16)], axis=1
    )
    shared_sum = reduce_dp(grad_shared)
    ffn_part = dot_nt(shared_hidden, shared_dn)
    h2_grad = dot_nt(shared_back, shared_gu)

    xe_own, xe_far = dispatch(h2)
    out_own, out_far, back_own, back_far, gate_grad_own, gate_grad_far, expert_sums = (
        [],
        [],
        [],
        [],
        [],
        [],
        [],
    )
    for s in range(half):
        weight = expert_full[s]
        w_gu, w_dn = weight[:, : 2 * e_cols], weight[:, 2 * e_cols :]
        inputs = jnp.concatenate([xe_own[s], xe_far[s]], axis=0)
        incoming = jnp.concatenate([go_own[s], go_far[s]], axis=0)
        gates = jnp.concatenate([gate_own[s], gate_far[s]], axis=0)[:, None]
        val = dot(inputs, w_gu)
        eg, eu = val[:, :e_cols], val[:, e_cols:]
        hidden = (jax.nn.silu(eg) * eu).astype(bf16).astype(f32)
        raw = dot(incoming, w_dn)
        gate_grad = jnp.sum(hidden * raw, axis=1)
        gated = (hidden * gates).astype(bf16)
        back = jnp.concatenate(silu_back(eg, eu, raw * gates), axis=1).astype(bf16)
        grad = jnp.concatenate([dot_tn(inputs, back, bf16), dot_tn(incoming, gated, bf16)], axis=1)
        expert_sums.append(chain_reduce(grad.reshape(nz, 2 * d_rows, 3 * e_cols)).astype(bf16))
        outs = dot_nt(gated, w_dn, bf16)
        backs = dot_nt(back, w_gu, bf16)
        out_own.append(outs[:capacity])
        out_far.append(outs[capacity:])
        back_own.append(backs[:capacity])
        back_far.append(backs[capacity:])
        gate_grad_own.append(gate_grad[:capacity])
        gate_grad_far.append(gate_grad[capacity:])
    back_here = jnp.concatenate([swap_core(b) for b in back_far], axis=0)
    out_here = jnp.concatenate([swap_core(b) for b in out_far], axis=0)
    gate_grad_here = swap_core(jnp.concatenate(gate_grad_far, axis=0))
    gate_grad_mine = jnp.concatenate(gate_grad_own, axis=0)

    h2_grad = (
        h2_grad + dot(own_hot, jnp.concatenate(back_own, axis=0)) + dot(far_hot, back_here)
    )
    h2_grad_here = sum_rows(blocks_of(h2_grad))
    gate_tokens = jnp.stack(
        [
            jnp.sum(
                jnp.where(flat_slot[:, k : k + 1] == own_ids[None, :], gate_grad_mine[None, :], 0.0)
                + jnp.where(
                    flat_slot[:, k : k + 1] == far_ids[None, :], gate_grad_here[None, :], 0.0
                ),
                axis=1,
            )
            for k in range(TOP)
        ],
        axis=1,
    )
    gates_here = sum_rows(blocks_of(gate_tokens))
    ffn_part = (
        ffn_part + dot(own_hot, jnp.concatenate(out_own, axis=0)) + dot(far_hot, out_here)
    )
    output = (middle + sum_rows(blocks_of(ffn_part))).astype(bf16)

    router_here = router[:local_rows]
    route_grad = gates_here * kept_mine[:local_rows]
    router_grad = jnp.sum(
        jnp.where(
            routes_mine[:local_rows, :, None] == expert_ids, route_grad[:, :, None], 0.0
        ),
        axis=1,
    )
    logit_grad = (
        router_here * (router_grad - jnp.sum(router_here * router_grad, axis=-1, keepdims=True))
    ).astype(bf16)
    grad_router = dot_tn(normed_two, logit_grad)
    h2_grad_here = h2_grad_here + dot_nt(logit_grad, router_full)
    middle_norm_grad, grad_gain_two = norm_back(middle, gain_two, h2_grad_here)
    middle_grad = out_grad.astype(f32) + middle_norm_grad
    attn_grad = jnp.concatenate(gather_rows(middle_grad.astype(bf16)), axis=0)

    out_sum = reduce_dp(dot_tn(attn_grad, attended, bf16))
    attended_grad = dot(attn_grad, out_full, out=bf16).reshape(rows, heads, VD)
    query_grad, nope_grad, rope_grad, value_grad = attend_backward(
        queries, key_nope, key_rope, values_all, log_total, attended_grad, allowed
    )
    query_grad = query_grad * query_scale
    query_raw_grad = (
        jnp.concatenate(
            [
                query_grad[..., :NOPE],
                rotate(query_grad[..., NOPE:], cosine[:, None, :], -sine_table[:, None, :]),
            ],
            axis=-1,
        )
        .astype(bf16)
        .reshape(rows, q_cols)
    )
    kv_grad = (
        jnp.concatenate([nope_grad, value_grad], axis=-1)
        .astype(bf16)
        .reshape(rows, heads * (NOPE + VD))
    )
    latent_grad = dot_nt(kv_grad, latent_up)
    latent_raw_grad, grad_gain_latent = norm_back(compressed[:, :KVR], gain_latent, latent_grad)
    compressed_grad = jnp.concatenate(
        [latent_raw_grad, rotate(rope_grad, cosine, -sine_table)], axis=-1
    )
    compressed_round = sum_rows(blocks_of(compressed_grad)).astype(bf16)
    kvup_sum = reduce_dp(dot_tn(latent, kv_grad, bf16))
    query_sum = reduce_dp(dot_tn(normed_all, query_raw_grad, bf16))
    normed_one = normed_all[:local_rows]
    grad_kvdown = dot_tn(normed_one, compressed_round)
    h1_grad = sum_rows(blocks_of(dot_nt(query_raw_grad, query_full))) + dot_nt(
        compressed_round, down_full
    )
    input_norm_grad, grad_gain_one = norm_back(x_here, gain_one, h1_grad)
    input_grad = middle_grad + input_norm_grad

    gain_latent_cols = jnp.pad(
        grad_gain_latent.reshape(-1, kv_gain.shape[0]),
        ((0, 0), (0, small_rows - kv_gain.shape[0])),
    ).reshape(-1)
    small_grad = jnp.concatenate(
        [
            grad_kvdown,
            grad_router,
            grad_gain_one[:, None],
            grad_gain_two[:, None],
            gain_latent_cols[:, None],
        ],
        axis=1,
    )
    small_grad = jnp.pad(small_grad, ((0, 0), (0, -small_grad.shape[1] % 128)))
    by_peer = small_grad.reshape(dp_count, peers, small_rows, small_grad.shape[1])
    small_sum = sum_rows(
        [
            lax.dynamic_index_in_dim(by_peer, me ^ k, 1, False).reshape(
                dp_count * small_rows, small_grad.shape[1]
            )
            for k in range(peers)
        ]
    )
    small_sum = reduce_dp(small_sum.astype(bf16))
    kv_out = small_sum[:, :kv_cols]
    router_out = small_sum[:, kv_cols : kv_cols + experts]
    gain_one_out = small_sum[:, kv_cols + experts]
    gain_two_out = small_sum[:, kv_cols + experts + 1]
    gain_latent_out = small_sum[: kv_gain.shape[0], kv_cols + experts + 2]

    mine = [
        lax.dynamic_index_in_dim(e.reshape(2, d_rows, 3 * e_cols), core, 0, False)
        for e in expert_sums
    ]
    theirs = [
        swap_core(lax.dynamic_index_in_dim(e.reshape(2, d_rows, 3 * e_cols), 1 - core, 0, False))
        for e in expert_sums
    ]
    expert_grad = jnp.stack(
        [jnp.where(first, a, b) for a, b in zip(mine, theirs)]
        + [jnp.where(first, b, a) for a, b in zip(mine, theirs)],
        axis=0,
    ).astype(f32)

    return (
        output,
        input_grad,
        gain_one_out,
        query_sum,
        kv_out,
        gain_latent_out,
        kvup_sum,
        out_sum.T,
        gain_two_out,
        router_out,
        shared_sum[:, :s_cols],
        shared_sum[:, s_cols : 2 * s_cols],
        shared_sum[:, 2 * s_cols :].T,
        expert_grad[:, :, :e_cols],
        expert_grad[:, :, e_cols : 2 * e_cols],
        jnp.swapaxes(expert_grad[:, :, 2 * e_cols :], 1, 2),
    )


def solution(mesh):
    placed = (
        P(("dp", "tensor"), None),
        P(("dp", "tensor"), None),
        P("dp", None),
        P("dp"),
        P("dp", None),
        P(("dp", "tensor")),
        P("dp", "tensor"),
        P(("dp", "tensor"), None),
        P(("dp", "tensor")),
        P("dp", "tensor"),
        P("tensor", "dp"),
        P(("dp", "tensor")),
        P(("dp", "tensor"), None),
        P("dp", "tensor"),
        P("dp", "tensor"),
        P("tensor", "dp"),
        P(None, "dp", "tensor"),
        P(None, "dp", "tensor"),
        P(None, "tensor", "dp"),
    )
    return jax.shard_map(
        on_device,
        mesh=mesh,
        in_specs=placed,
        out_specs=(
            P(("dp", "tensor"), None),
            P(("dp", "tensor"), None),
            P(("dp", "tensor")),
            P("dp", "tensor"),
            P(("dp", "tensor"), None),
            P(("dp", "tensor")),
            P("dp", "tensor"),
            P("tensor", "dp"),
            P(("dp", "tensor")),
            P(("dp", "tensor"), None),
            P("dp", "tensor"),
            P("dp", "tensor"),
            P("tensor", "dp"),
            P(None, "dp", "tensor"),
            P(None, "dp", "tensor"),
            P(None, "tensor", "dp"),
        ),
        check_vma=False,
    )
```

```python
import functools

import jax
import jax.numpy as jnp
from jax import lax
from jax.experimental import pallas as pl
from jax.experimental.pallas import tpu as pltpu
from jax.sharding import PartitionSpec as P

D = 2048
NOPE = 128
ROPE = 64
VD = 128
KVR = 512
TOP = 2
LENGTH = 1024

eps = 1e-06
bf16 = jnp.bfloat16
f32 = jnp.float32


def dot(a, b, dims=((1,), (0,)), out=f32):
    return lax.dot_general(a, b, (dims, ((), ())), preferred_element_type=f32).astype(out)


def dot_nt(a, b, out=f32):
    return dot(a, b, ((1,), (1,)), out)


def dot_tn(a, b, out=f32):
    return dot(a, b, ((0,), (0,)), out)


def inv_rms(values):
    return lax.rsqrt(jnp.mean(values * values, axis=-1, keepdims=True) + eps)


def norm_rows(values, gain_vec):
    return values * inv_rms(values) * gain_vec


def norm_back(values, gain_vec, upstream):
    inv = inv_rms(values)
    scaled = upstream * gain_vec
    grad = inv * scaled - values * (
        inv * inv * inv * jnp.mean(values * scaled, axis=-1, keepdims=True)
    )
    return grad, jnp.sum(upstream * values * inv, axis=0)


def swap_core(values):
    count = lax.axis_size("dp")
    return lax.ppermute(values, "dp", [(i, i ^ 1) for i in range(count)])


def gather_rows(values):
    count = lax.axis_size("tensor")
    return [values] + [
        lax.ppermute(values, "tensor", [(i, i ^ k) for i in range(count)])
        for k in range(count - 1, 0, -1)
    ][::-1]


def send_back(part, k):
    count = lax.axis_size("tensor")
    return part if k == 0 else lax.ppermute(part, "tensor", [(i, i ^ k) for i in range(count)])


def sum_rows(blocks):
    count = lax.axis_size("tensor")
    total = blocks[0].astype(f32)
    arrived = [
        lax.ppermute(blocks[k].astype(bf16), "tensor", [(i, i ^ k) for i in range(count)])
        for k in range(count - 1, 0, -1)
    ]
    for piece in arrived:
        total = total + piece.astype(f32)
    return total


NT=(((1,),(1,)),((),())); NN=(((1,),(0,)),((),()))
def mm(a,b,dims=NN): return lax.dot_general(a,b,dims,preferred_element_type=f32)

def ffn_kernel(parts, hidden_cols, *refs):
    x_refs=refs[:parts]; g_refs=refs[parts:2*parts]; gate_ref, w_ref = refs[2*parts:2*parts+2]
    outs=refs[2*parts+2:]
    out_refs=outs[:parts]; back_refs=outs[parts:2*parts]; grad_ref, dgate_ref = outs[2*parts:2*parts+2]
    val, raw, back_t, gated_t, back_n, gated_n = outs[2*parts+2:]
    phase=pl.program_id(0); step=pl.program_id(1)
    F=hidden_cols
    def rows_of(rs):
        pieces=[r[...].reshape(r.shape[-2:]) for r in rs]
        return pieces[0] if parts==1 else jnp.concatenate(pieces,axis=0)
    x=rows_of(x_refs); g=rows_of(g_refs)
    w=w_ref[...].reshape(w_ref.shape[-2:])
    @pl.when(phase==0)
    def _():
        a=mm(w[:2*F],x,NT); b=mm(w[2*F:],g,NT)
        @pl.when(step==0)
        def _():
            val[...]=a; raw[...]=b
        @pl.when(step>0)
        def _():
            val[...]+=a; raw[...]+=b
    @pl.when((phase==1)&(step==0))
    def _():
        eg=val[:F]; eu=val[F:]; r=raw[...]; gate=gate_ref[...]
        s=jax.nn.sigmoid(eg); act=eg*s
        hid=(act*eu).astype(bf16).astype(f32)
        dgate_ref[...]=jnp.sum(hid*r,axis=0,keepdims=True)
        gated=(hid*gate).astype(bf16)
        d=r*gate
        bg=(d*eu*s*(1.0+eg*(1.0-s))).astype(bf16); bu=(d*act).astype(bf16)
        back_t[:F]=bg; back_t[F:]=bu; gated_t[...]=gated
        back_n[...]=back_t[...].T; gated_n[...]=gated.T
    @pl.when(phase==1)
    def _():
        o=mm(gated_n[...],w[2*F:]); b=mm(back_n[...],w[:2*F])
        at=0
        for ro,rb in zip(out_refs,back_refs):
            n=ro.shape[-2]
            ro[...]=o[at:at+n].astype(ro.dtype).reshape(ro.shape); rb[...]=b[at:at+n].astype(rb.dtype).reshape(rb.shape); at+=n
        sh=grad_ref.shape[:-2]
        gr=jnp.concatenate([mm(back_t[...],x),mm(gated_t[...],g)],axis=0).astype(bf16)
        grad_ref[...]=gr.reshape(grad_ref.shape)

def ffn(xs, gs, gates, w, stage, out_dtype):
    parts=len(xs)
    F=w.shape[-2]//3; dl=w.shape[-1]
    D=xs[0].shape[-1]; nd=D//dl
    ns=[x.shape[-2] for x in xs]; n=sum(ns)
    if stage is None:
        row_spec=[pl.BlockSpec((m,dl),lambda p,j:(0,j)) for m in ns]
        w_spec=pl.BlockSpec((1,3*F,dl),lambda p,j:(j,0,0))
        g_shape=(nd,3*F,dl); g_spec=pl.BlockSpec((1,3*F,dl),lambda p,j:(j*p,0,0))
    else:
        row_spec=[pl.BlockSpec((1,m,dl),lambda p,j:(stage,0,j)) for m in ns]
        ws=stage%w.shape[1]
        w_spec=pl.BlockSpec((1,1,1,3*F,dl),lambda p,j:(j//2,ws,j%2,0,0))
        g_shape=(nd//2,2,3*F,dl); g_spec=pl.BlockSpec((1,1,3*F,dl),lambda p,j:((j*p)//2,(j*p)%2,0,0))
    out_spec=[pl.BlockSpec((m,dl),lambda p,j:(0,j*p)) for m in ns]
    flops=2*n*D*F*9
    res = pl.pallas_call(
        functools.partial(ffn_kernel,parts,F),
        grid=(2,nd),
        in_specs=row_spec*2+[pl.BlockSpec((1,n),lambda p,j:(0,0)),w_spec],
        out_specs=out_spec*2+[g_spec,pl.BlockSpec((1,n),lambda p,j:(0,0))],
        out_shape=[jax.ShapeDtypeStruct((m,D),out_dtype) for m in ns]*2+[jax.ShapeDtypeStruct(g_shape,bf16),jax.ShapeDtypeStruct((1,n),f32)],
        scratch_shapes=[pltpu.VMEM((2*F,n),f32),pltpu.VMEM((F,n),f32),pltpu.VMEM((2*F,n),bf16),pltpu.VMEM((F,n),bf16),pltpu.VMEM((n,2*F),bf16),pltpu.VMEM((n,F),bf16)],
        compiler_params=pltpu.CompilerParams(dimension_semantics=("arbitrary","arbitrary"),vmem_limit_bytes=60*1024*1024),
        cost_estimate=pl.CostEstimate(flops=flops,bytes_accessed=2*3*F*D*3+2*n*D*6,transcendentals=n*F),
        name="ffn",
    )(*xs,*gs,gates,w)
    return res[:parts], res[parts:2*parts], res[2*parts], res[2*parts+1]


def front_kernel(sizes, x_ref, w_ref, cos_ref, sin_ref, gl_ref, h_ref, qn_ref, qr_ref, comp_ref, lat_ref, kr_ref, kv_ref, extra, ups):
    heads, at_q, at_kv, at_gain, at_up, chunks, up_rows, scale = sizes
    nd, _, dl = w_ref.shape
    qn_cols, qr_cols = heads * NOPE, heads * ROPE
    half = ROPE // 2
    main = qn_cols + qr_cols + KVR

    @pl.when(pl.program_id(0) == 0)
    def _():
        for j in range(nd):
            w_r = w_ref[j, at_q + qn_cols : at_q + qn_cols + qr_cols, :]
            w_k = w_ref[j, at_kv + KVR : at_kv + KVR + ROPE, :]
            swapped = []
            for h in range(heads):
                swapped.append(w_r[h * ROPE + half : (h + 1) * ROPE])
                swapped.append(w_r[h * ROPE : h * ROPE + half])
            extra[j] = jnp.concatenate(
                swapped + [w_k, w_k, w_k[half:], w_k[:half], w_k[half:], w_k[:half]], axis=0
            )
            for c in range(chunks):
                at = at_up + c * up_rows
                ups[c, j * up_rows : (j + 1) * up_rows, :] = w_ref[j, at : at + up_rows, :]

    x = x_ref[...].astype(f32)
    inv = lax.rsqrt(jnp.mean(x * x, axis=-1, keepdims=True) + eps)
    acc = None
    for j in range(nd):
        gain = w_ref[j, at_gain : at_gain + 16, :][0:1].astype(f32)
        h = (x[:, j * dl : (j + 1) * dl] * inv * gain).astype(bf16)
        h_ref[:, j * dl : (j + 1) * dl] = h
        part = [mm(h, w_ref[j, at_q : at_q + main, :], NT), mm(h, extra[j], NT)]
        acc = part if acc is None else [a + b for a, b in zip(acc, part)]
    a, b = acc
    cos, sin = cos_ref[...], sin_ref[...]
    qn_ref[...] = (a[:, :qn_cols] * scale).astype(bf16)
    qr_ref[...] = (
        (a[:, qn_cols : qn_cols + qr_cols] * cos + b[:, :qr_cols] * sin) * scale
    ).astype(bf16)
    comp = a[:, qn_cols + qr_cols :]
    comp_ref[...] = comp
    wide = 2 * ROPE
    kr_ref[...] = (
        b[:, qr_cols : qr_cols + wide] * cos[:, :wide]
        + b[:, qr_cols + wide : qr_cols + 2 * wide] * sin[:, :wide]
    ).astype(bf16)
    lat = (
        comp * lax.rsqrt(jnp.mean(comp * comp, axis=-1, keepdims=True) + eps) * gl_ref[...]
    ).astype(bf16)
    lat_ref[...] = lat
    for c in range(chunks):
        kv_ref[:, c * dl : (c + 1) * dl] = mm(lat, ups[c]).astype(bf16)


def front(x, w, cos, sin, gain_latent, sizes):
    heads, at_q, at_kv, at_gain, at_up, chunks, up_rows, scale = sizes
    rows, width = x.shape
    nd, _, dl = w.shape
    tb = min(256, rows)
    row = lambda cols: pl.BlockSpec((tb, cols), lambda i: (i, 0))
    whole = lambda a: pl.BlockSpec(a.shape, lambda i: (0,) * a.ndim)
    cols = [width, heads * NOPE, heads * ROPE, KVR, KVR, 2 * ROPE, heads * (NOPE + VD)]
    kinds = [bf16, bf16, bf16, f32, bf16, bf16, bf16]
    return pl.pallas_call(
        functools.partial(front_kernel, sizes),
        grid=(rows // tb,),
        in_specs=[row(width), whole(w), row(heads * ROPE), row(heads * ROPE), whole(gain_latent)],
        out_specs=[row(c) for c in cols],
        out_shape=[jax.ShapeDtypeStruct((rows, c), k) for c, k in zip(cols, kinds)],
        scratch_shapes=[
            pltpu.VMEM((nd, heads * ROPE + 4 * ROPE, dl), bf16),
            pltpu.VMEM((chunks, nd * up_rows, dl), bf16),
        ],
        compiler_params=pltpu.CompilerParams(vmem_limit_bytes=60 * 1024 * 1024),
        cost_estimate=pl.CostEstimate(
            flops=2 * rows * width * 1900, bytes_accessed=2 * w.size + 12 * rows * width, transcendentals=0
        ),
        name="front",
    )(x, w, cos, sin, gain_latent)


def head_rope(wide, h):
    lane = lax.broadcasted_iota(jnp.int32, wide.shape, 1)
    return jnp.where((lane // ROPE) == (h % 2), wide, jnp.zeros_like(wide))


def attend_kernel(heads, qn_ref, qr_ref, kr_ref, kv_ref, kpos_ref, lim_ref, w_ref, att_ref, out_ref):
    kr = kr_ref[...]
    keep = kpos_ref[...] <= lim_ref[...]
    wide = 2 * ROPE
    for h in range(heads):
        at = h * (NOPE + VD)
        q = jnp.concatenate(
            [
                qn_ref[:, h * NOPE : (h + 1) * NOPE],
                head_rope(qr_ref[:, (h // 2) * wide : (h // 2 + 1) * wide], h),
            ],
            axis=1,
        )
        k = jnp.concatenate([kv_ref[:, at : at + NOPE], kr], axis=1)
        s = jnp.where(keep, mm(q, k, NT), -1e30)
        p = jnp.exp(s - jnp.max(s, axis=1, keepdims=True))
        p = (p * (1.0 / jnp.sum(p, axis=1, keepdims=True))).astype(bf16)
        att_ref[:, h * VD : (h + 1) * VD] = mm(p, kv_ref[:, at + NOPE : at + NOPE + VD]).astype(bf16)
    att = att_ref[...]
    dl = w_ref.shape[2]
    for j in range(w_ref.shape[0]):
        out_ref[:, j * dl : (j + 1) * dl] = mm(att, w_ref[j]).astype(out_ref.dtype)


def attend(qn, qr, kr, kv, kpos, limit, w, block, block_rows, out_dtype):
    rows = qn.shape[0]
    heads = qn.shape[1] // NOPE
    nd, _, dl = w.shape
    row = lambda cols: pl.BlockSpec((block_rows, cols), lambda i: (block, 0))
    whole = lambda a: pl.BlockSpec(a.shape, lambda i: (0,) * a.ndim)
    first = lambda cols: pl.BlockSpec((block_rows, cols), lambda i: (0, 0))
    return pl.pallas_call(
        functools.partial(attend_kernel, heads),
        grid=(1,),
        in_specs=[
            row(heads * NOPE),
            row(heads * ROPE),
            whole(kr),
            whole(kv),
            whole(kpos),
            row(1),
            pl.BlockSpec((nd, heads * VD, dl), lambda i: (0, 0, 0)),
        ],
        out_specs=[first(heads * VD), first(nd * dl)],
        out_shape=[
            jax.ShapeDtypeStruct((block_rows, heads * VD), bf16),
            jax.ShapeDtypeStruct((block_rows, nd * dl), out_dtype),
        ],
        compiler_params=pltpu.CompilerParams(vmem_limit_bytes=60 * 1024 * 1024),
        cost_estimate=pl.CostEstimate(
            flops=2 * block_rows * heads * (rows * 384 + VD * nd * dl),
            bytes_accessed=8 * 1024 * 1024,
            transcendentals=block_rows * heads * rows,
        ),
        name="attend",
    )(qn, qr, kr, kv, kpos, limit, w)


def rot_back(v, cos, sin):
    half = ROPE // 2
    lane = lax.broadcasted_iota(jnp.int32, v.shape, 1)
    width = v.shape[1]
    down = pltpu.roll(v, width - half, 1)
    up = pltpu.roll(v, half, 1)
    other = jnp.where(lane % ROPE < half, down, up)
    return v * cos - other * sin


def attend_back_kernel(heads, scale, first, *refs):
    da_ref, qn_ref, qr_ref, kr_ref, kv_ref, kpos_ref, lim_ref, cos_ref, sin_ref = refs[:9]
    wo_ref, wa_ref, wb_ref, wr_ref = refs[9:13]
    dkv_in, dkr_in = (None, None) if first else refs[13:15]
    dq_ref, dh_ref, dkv_ref, dkr_ref = refs[13 if first else 15 :]
    nd, _, dl = wo_ref.shape
    wide = 2 * ROPE
    width = NOPE + VD
    grad = None
    for j in range(nd):
        part = mm(da_ref[:, j * dl : (j + 1) * dl], wo_ref[j], NT)
        grad = part if grad is None else grad + part
    grad = grad.astype(bf16)
    kr = kr_ref[...]
    keep = kpos_ref[...] <= lim_ref[...]
    rope_grads = []
    dkr = jnp.zeros(dkr_ref.shape, f32) if first else dkr_in[...]
    for h in range(heads):
        at = h * width
        q = jnp.concatenate(
            [
                qn_ref[:, h * NOPE : (h + 1) * NOPE],
                head_rope(qr_ref[:, (h // 2) * wide : (h // 2 + 1) * wide], h),
            ],
            axis=1,
        )
        k = jnp.concatenate([kv_ref[:, at : at + NOPE], kr], axis=1)
        do = grad[:, h * VD : (h + 1) * VD]
        s = jnp.where(keep, mm(k, q, NT), -1e30)
        p = jnp.exp(s - jnp.max(s, axis=0, keepdims=True))
        p = p * (1.0 / jnp.sum(p, axis=0, keepdims=True))
        dp = mm(kv_ref[:, at + NOPE : at + width], do, NT)
        ds = (p * (dp - jnp.sum(p * dp, axis=0, keepdims=True))).astype(bf16)
        dv = mm(p.astype(bf16), do)
        dk = mm(ds, q)
        if first:
            dkv_ref[:, at : at + NOPE] = dk[:, :NOPE]
            dkv_ref[:, at + NOPE : at + width] = dv
        else:
            dkv_ref[:, at : at + NOPE] = dkv_in[:, at : at + NOPE] + dk[:, :NOPE]
            dkv_ref[:, at + NOPE : at + width] = dkv_in[:, at + NOPE : at + width] + dv
        dkr = dkr + dk[:, NOPE:]
        dq = lax.dot_general(ds, k, (((0,), (0,)), ((), ())), preferred_element_type=f32)
        dq_ref[:, h * NOPE : (h + 1) * NOPE] = (dq[:, :NOPE] * scale).astype(bf16)
        masked = head_rope(dq[:, NOPE:], h)
        if h % 2:
            rope_grads[-1] = rope_grads[-1] + masked
        else:
            rope_grads.append(masked)
    dkr_ref[...] = dkr
    ropes = rope_grads[0] if len(rope_grads) == 1 else jnp.concatenate(rope_grads, axis=1)
    at = heads * NOPE
    dq_ref[:, at:] = (rot_back(ropes, cos_ref[...], sin_ref[...]) * scale).astype(bf16)
    half = at // 2
    for j in range(nd):
        dh_ref[:, j * dl : (j + 1) * dl] = (
            mm(dq_ref[:, :half], wa_ref[j])
            + mm(dq_ref[:, half:at], wb_ref[j])
            + mm(dq_ref[:, at:], wr_ref[j])
        ).astype(dh_ref.dtype)


def attend_back(da, qn, qr, kr, kv, kpos, limit, cos, sin, w, so_far, block, scale, out_dtype):
    block_rows = da.shape[0]
    rows = qn.shape[0]
    heads = qn.shape[1] // NOPE
    nd, _, dl = w.shape
    row = lambda cols: pl.BlockSpec((block_rows, cols), lambda i: (block, 0))
    whole = lambda a: pl.BlockSpec(a.shape, lambda i: (0,) * a.ndim)
    rows_w = lambda size, at: pl.BlockSpec((nd, size, dl), lambda i: (0, at, 0))
    part = heads * ROPE
    dkv = jax.ShapeDtypeStruct((rows, heads * (NOPE + VD)), f32)
    dkr = jax.ShapeDtypeStruct((rows, 2 * ROPE), f32)
    first = so_far is None
    return pl.pallas_call(
        functools.partial(attend_back_kernel, heads, scale, first),
        grid=(1,),
        in_specs=[
            whole(da),
            row(heads * NOPE),
            row(heads * ROPE),
            whole(kr),
            whole(kv),
            whole(kpos),
            pl.BlockSpec((1, block_rows), lambda i: (0, block)),
            row(heads * ROPE),
            row(heads * ROPE),
            rows_w(2 * part, 0),
            rows_w(part, 2),
            rows_w(part, 3),
            rows_w(part, 4),
        ]
        + ([] if first else [whole(dkv), whole(dkr)]),
        out_specs=[
            pl.BlockSpec((block_rows, 3 * part), lambda i: (0, 0)),
            pl.BlockSpec((block_rows, nd * dl), lambda i: (0, 0)),
            whole(dkv),
            whole(dkr),
        ],
        out_shape=[
            jax.ShapeDtypeStruct((block_rows, 3 * part), bf16),
            jax.ShapeDtypeStruct((block_rows, nd * dl), out_dtype),
            dkv,
            dkr,
        ],
        input_output_aliases={} if first else {13: 2, 14: 3},
        compiler_params=pltpu.CompilerParams(vmem_limit_bytes=60 * 1024 * 1024),
        cost_estimate=pl.CostEstimate(
            flops=2 * block_rows * heads * (rows * 1024 + 5 * ROPE * nd * dl),
            bytes_accessed=20 * 1024 * 1024,
            transcendentals=block_rows * heads * rows,
        ),
        name="attend_back",
    )(da, qn, qr, kr, kv, kpos, limit, cos, sin, w, w, w, w, *(() if first else so_far))


def latent_back_kernel(sizes, dkv_ref, dkr_ref, comp_ref, cos_ref, sin_ref, gl_ref, w_ref, dkvb_ref, dc_ref, dg_ref, ups):
    chunks, up_rows, in_rows = sizes
    nd, _, dl = w_ref.shape
    dkv = dkv_ref[...].astype(bf16)
    dkvb_ref[...] = dkv

    @pl.when(pl.program_id(0) == 0)
    def _():
        for j in range(nd):
            for c in range(chunks):
                at = in_rows + c * up_rows
                ups[c, j * up_rows : (j + 1) * up_rows, :] = w_ref[j, at : at + up_rows, :]

    dlat = None
    for c in range(chunks):
        part = mm(dkv[:, c * dl : (c + 1) * dl], ups[c], NT)
        dlat = part if dlat is None else dlat + part
    comp = comp_ref[...]
    inv = lax.rsqrt(jnp.mean(comp * comp, axis=-1, keepdims=True) + eps)
    scaled = dlat * gl_ref[...]
    dc_ref[:, :KVR] = (
        inv * scaled - comp * (inv * inv * inv * jnp.mean(comp * scaled, axis=-1, keepdims=True))
    ).astype(dc_ref.dtype)
    dg = jnp.sum(dlat * comp * inv, axis=0, keepdims=True)

    @pl.when(pl.program_id(0) == 0)
    def _():
        dg_ref[...] = dg

    @pl.when(pl.program_id(0) > 0)
    def _():
        dg_ref[...] += dg

    dkr = dkr_ref[...]
    dkr = dkr + pltpu.roll(dkr, ROPE, 1)
    wide = 2 * ROPE
    dkr = rot_back(dkr, cos_ref[:, :wide], sin_ref[:, :wide])
    lane = lax.broadcasted_iota(jnp.int32, dkr.shape, 1)
    dc_ref[:, KVR:] = jnp.where(lane < ROPE, dkr, 0.0).astype(dc_ref.dtype)


def latent_back(dkv, dkr, comp, cos, sin, gain_latent, w, at_up, chunks, up_rows):
    rows = dkv.shape[0]
    nd, _, dl = w.shape
    tb = min(256, rows)
    row = lambda cols: pl.BlockSpec((tb, cols), lambda i: (i, 0))
    whole = lambda a: pl.BlockSpec(a.shape, lambda i: (0,) * a.ndim)
    return pl.pallas_call(
        functools.partial(latent_back_kernel, (chunks, up_rows, at_up)),
        grid=(rows // tb,),
        in_specs=[
            row(dkv.shape[1]),
            row(dkr.shape[1]),
            row(KVR),
            row(cos.shape[1]),
            row(cos.shape[1]),
            whole(gain_latent),
            whole(w),
        ],
        out_specs=[row(dkv.shape[1]), row(KVR + 2 * ROPE), pl.BlockSpec((1, KVR), lambda i: (0, 0))],
        out_shape=[
            jax.ShapeDtypeStruct(dkv.shape, bf16),
            jax.ShapeDtypeStruct((rows, KVR + 2 * ROPE), bf16),
            jax.ShapeDtypeStruct((1, KVR), f32),
        ],
        scratch_shapes=[pltpu.VMEM((chunks, nd * up_rows, dl), bf16)],
        compiler_params=pltpu.CompilerParams(vmem_limit_bytes=60 * 1024 * 1024),
        cost_estimate=pl.CostEstimate(
            flops=2 * rows * KVR * dkv.shape[1], bytes_accessed=16 * 1024 * 1024, transcendentals=0
        ),
        name="latent_back",
    )(dkv, dkr, comp, cos, sin, gain_latent, w)


def outer_kernel(parts, *refs):
    a_refs, b_refs, out_ref, at_ref = refs[:parts], refs[parts : 2 * parts], refs[-2], refs[-1]

    @pl.when(pl.program_id(0) == 0)
    def _():
        at = 0
        for a in a_refs:
            at_ref[:, at : at + a.shape[0]] = a[...].T
            at += a.shape[0]

    right = b_refs[0][...] if parts == 1 else jnp.concatenate([b[...] for b in b_refs], axis=0)
    out_ref[...] = mm(at_ref[...], right).astype(bf16)[None]


def outer(left, right, width):
    parts = len(left)
    rows = sum(a.shape[0] for a in left)
    cols = left[0].shape[1]
    count = right[0].shape[1] // width
    return pl.pallas_call(
        functools.partial(outer_kernel, parts),
        grid=(count,),
        in_specs=[pl.BlockSpec(a.shape, lambda j: (0, 0)) for a in left]
        + [pl.BlockSpec((b.shape[0], width), lambda j: (0, j)) for b in right],
        out_specs=pl.BlockSpec((1, cols, width), lambda j: (j, 0, 0)),
        out_shape=jax.ShapeDtypeStruct((count, cols, width), bf16),
        scratch_shapes=[pltpu.VMEM((cols, rows), bf16)],
        compiler_params=pltpu.CompilerParams(vmem_limit_bytes=60 * 1024 * 1024),
        cost_estimate=pl.CostEstimate(
            flops=2 * rows * cols * count * width,
            bytes_accessed=2 * (rows * cols + (rows + cols) * count * width),
            transcendentals=0,
        ),
        name="outer",
    )(*left, *right)


def after(values, *others):
    return lax.optimization_barrier((values, *others))[0]


class Chain:
    def __init__(self, blocks):
        self.blocks = blocks
        self.nz = lax.axis_size("dp") // 2
        self.place = lax.axis_index("dp") // 2
        self.rising = self.falling = None
        self.done = 0
        self.advance()

    def advance(self, *others):
        nz, place, step = self.nz, self.place, self.done
        if step >= nz - 1:
            return
        up = lax.dynamic_index_in_dim(self.blocks, jnp.clip(nz - 1 - step + place, 0, nz - 1), 0, False)
        down = lax.dynamic_index_in_dim(self.blocks, jnp.clip(step - nz + 1 + place, 0, nz - 1), 0, False)
        if step > 0:
            up = (up.astype(f32) + self.rising.astype(f32)).astype(bf16)
            down = (down.astype(f32) + self.falling.astype(f32)).astype(bf16)
        self.sent = (up, down)
        self.rising = lax.ppermute(
            up,
            "dp",
            [(2 * j + c, 2 * j + 2 + c) for j in range(nz - 1) if j <= step for c in range(2)],
        )
        self.falling = lax.ppermute(
            down,
            "dp",
            [(2 * j + c, 2 * j - 2 + c) for j in range(1, nz) if nz - 1 - j <= step for c in range(2)],
        )
        self.done += 1

    def rest(self):
        while self.done < self.nz - 1:
            self.advance()

    def result(self):
        self.rest()
        mine = lax.dynamic_index_in_dim(self.blocks, self.place, 0, False).astype(f32)
        return mine + self.rising.astype(f32) + self.falling.astype(f32)


def chain_dp(grad):
    count = lax.axis_size("dp")
    core = lax.axis_index("dp") % 2
    parts = grad.reshape(count // 2, 2, grad.shape[1], grad.shape[2])
    other = lax.dynamic_index_in_dim(parts, 1 - core, 1, False)
    mine = lax.dynamic_index_in_dim(parts, core, 1, False)
    return Chain((mine.astype(f32) + swap_core(other).astype(f32)).astype(bf16))


def on_device(
    block_input,
    out_grad,
    routes,
    prefixes,
    drop_order,
    attn_gain,
    query_proj,
    kv_down,
    kv_gain,
    kv_up,
    out_proj,
    ffn_gain,
    router_proj,
    shared_gate,
    shared_up,
    shared_down,
    expert_gate,
    expert_up,
    expert_down,
):
    me = lax.axis_index("tensor")
    place = lax.axis_index("dp")
    core = place % 2
    peers = lax.axis_size("tensor")
    dp_count = lax.axis_size("dp")
    nz = dp_count // 2
    local_rows = block_input.shape[0]
    rows = routes.shape[0]
    experts = expert_gate.shape[0]
    half = experts // 2
    capacity = rows * TOP * 9 // (8 * experts)
    qk_width = NOPE + ROPE
    query_scale = qk_width ** (-0.5)
    q_cols = query_proj.shape[1]
    heads = q_cols // qk_width
    d_rows = query_proj.shape[0]
    s_cols = shared_gate.shape[1]
    e_cols = expert_gate.shape[2]

    def in_order(array):
        return jnp.concatenate(
            [
                lax.dynamic_slice_in_dim(array, (me ^ k) * local_rows, local_rows, 0)
                for k in range(peers)
            ],
            axis=0,
        )

    small_rows = kv_down.shape[0]

    def column(vector):
        return jnp.pad(vector, (0, small_rows - vector.shape[0]))[:, None]

    small = jnp.concatenate(
        [kv_down, router_proj, column(attn_gain), column(ffn_gain), column(kv_gain)], axis=1
    )
    kv_cols = kv_down.shape[1]
    small_count = small.shape[1] + (-small.shape[1] % 16)
    small = jnp.pad(small, ((0, 0), (0, -small.shape[1] % 128)))
    small_blocks = gather_rows(small)
    x_all = jnp.concatenate(gather_rows(after(block_input, small)), axis=0)
    go_blocks = gather_rows(after(out_grad, x_all))
    go_all = jnp.concatenate(go_blocks, axis=0)

    small_all = jnp.zeros((peers * small_rows, small.shape[1]), bf16)
    for k, block in enumerate(small_blocks):
        small_all = lax.dynamic_update_slice_in_dim(small_all, block, (me ^ k) * small_rows, 0)
    by_head = query_proj.reshape(d_rows, heads, qk_width)
    up_rows = kv_up.shape[0]
    chunks = kv_up.shape[1] // d_rows
    front_local = jnp.concatenate(
        [
            out_proj,
            by_head[:, :, :NOPE].reshape(d_rows, heads * NOPE).T,
            by_head[:, :, NOPE:].reshape(d_rows, heads * ROPE).T,
            small_all[:, :small_count].T,
            jnp.swapaxes(kv_up.reshape(up_rows, chunks, d_rows), 0, 1).reshape(-1, d_rows),
        ],
        axis=0,
    )
    at_q = heads * VD
    at_kv = at_q + q_cols
    at_router = at_kv + kv_cols
    at_gain = at_router + experts
    at_up = at_kv + small_count
    weight_front = lax.all_gather(front_local, "dp", axis=0)
    router_full = jnp.swapaxes(weight_front[:, at_router:at_gain, :], 0, 1).reshape(experts, D)
    gain_one = weight_front[:, at_gain, :].reshape(1, D).astype(f32)
    gain_two = weight_front[:, at_gain + 1, :].reshape(1, D).astype(f32)
    gain_latent = (
        weight_front[:, at_gain + 2, :]
        .reshape(-1, small_rows)[:, : kv_gain.shape[0]]
        .reshape(1, KVR)
        .astype(f32)
    )
    shared_full = lax.all_gather(
        jnp.concatenate([shared_gate.T, shared_up.T, shared_down], axis=0), "dp", axis=0
    )

    expert_local = jnp.concatenate(
        [jnp.swapaxes(expert_gate, 1, 2), jnp.swapaxes(expert_up, 1, 2), expert_down], axis=1
    )
    kept_part = lax.dynamic_slice_in_dim(expert_local, core * half, half, 0)
    sent_part = lax.dynamic_slice_in_dim(expert_local, (1 - core) * half, half, 0)
    got_part = swap_core(sent_part)
    first = core == 0
    pair_part = jnp.stack(
        [jnp.where(first, kept_part, got_part), jnp.where(first, got_part, kept_part)], axis=1
    )
    groups = [[2 * j + c for j in range(nz)] for c in range(2)]
    per_gather = 2
    expert_full = [
        lax.all_gather(pair_part[s : s + per_gather], "dp", axis=0, axis_index_groups=groups)
        for s in range(0, half, per_gather)
    ]

    token_ids = jnp.arange(rows, dtype=jnp.int32)
    ranking = jnp.sum(
        jnp.where(drop_order[0][:, None] == token_ids[None, :], token_ids[:, None], 0), axis=0
    )
    expert_ids = jnp.arange(experts, dtype=jnp.int32)
    chosen = jnp.sum((routes[:, :, None] == expert_ids).astype(f32), axis=1)
    earlier = (ranking[None, :] < ranking[:, None]).astype(bf16)
    before = dot(earlier, chosen.astype(bf16)).astype(jnp.int32)
    slot_rank = jnp.sum(
        jnp.where(routes[:, :, None] == expert_ids, before[:, None, :], 0), axis=2
    )
    kept_mask = slot_rank < capacity
    flat_slot = in_order(jnp.where(kept_mask, routes * capacity + slot_rank, -1))
    routes_mine = in_order(routes)
    kept_mine = (flat_slot >= 0).astype(f32)
    slots = half * capacity
    slot_ids = jnp.arange(slots, dtype=jnp.int32)
    own_ids = core * slots + slot_ids
    far_ids = (1 - core) * slots + slot_ids

    def one_hot(ids):
        return (
            (flat_slot[:, 0:1] == ids[None, :]) | (flat_slot[:, 1:2] == ids[None, :])
        ).astype(bf16)

    own_hot = one_hot(own_ids)
    far_hot = one_hot(far_ids)

    def dispatch(values):
        return (
            dot_tn(own_hot, values, bf16).reshape(half, capacity, D),
            swap_core(dot_tn(far_hot, values, bf16)).reshape(half, capacity, D),
        )

    go_own, go_far = dispatch(go_all)

    places = in_order(token_ids)
    half_width = ROPE // 2
    frequency = jnp.exp(
        -jnp.log(10000.0) * jnp.arange(half_width, dtype=jnp.int32).astype(f32) / half_width
    )
    angles = places.astype(f32)[:, None] * frequency[None, :]
    cosine, sine = jnp.cos(angles), jnp.sin(angles)
    cos_wide = jnp.tile(jnp.concatenate([cosine, cosine], axis=1), (1, heads))
    sin_wide = jnp.tile(jnp.concatenate([-sine, sine], axis=1), (1, heads))
    limit = jnp.maximum(places, prefixes[0] - 1)

    sizes = (heads, at_q, at_kv, at_gain, at_up, chunks, up_rows, query_scale)
    normed_all, q_nope, q_rope, compressed, latent, key_rope, key_value = front(
        x_all, weight_front, cos_wide, sin_wide, gain_latent, sizes
    )
    attended = [None] * peers
    out_parts = [None] * peers
    for k in list(range(peers - 1, -1, -1)):
        attended[k], part = attend(
            q_nope,
            q_rope,
            key_rope,
            key_value,
            places[None, :],
            limit[:, None],
            weight_front,
            k,
            local_rows,
            bf16 if k else f32,
        )
        out_parts[k] = send_back(part, k)

    x_here = block_input.astype(f32)
    middle = x_here + sum(part.astype(f32) for part in out_parts)
    normed_two = norm_rows(middle, gain_two).astype(bf16)
    h2 = jnp.concatenate(gather_rows(normed_two), axis=0)

    def blocks_of(array):
        return [array[k * local_rows : (k + 1) * local_rows] for k in range(peers)]

    router = jax.nn.softmax(dot_nt(h2, router_full), axis=-1)
    route_gates = jnp.sum(
        jnp.where(routes_mine[:, :, None] == expert_ids, router[:, None, :], 0.0), axis=2
    )

    def slot_gates(ids):
        return jnp.sum(
            jnp.where(flat_slot[:, 0:1] == ids[None, :], route_gates[:, 0:1], 0.0)
            + jnp.where(flat_slot[:, 1:2] == ids[None, :], route_gates[:, 1:2], 0.0),
            axis=0,
        )

    gate_own = slot_gates(own_ids).reshape(half, capacity)
    gate_far = swap_core(slot_gates(far_ids).reshape(half, capacity))

    (ffn_part,), (h2_grad,), grad_shared, _ = ffn(
        [h2], [go_all], jnp.ones((1, rows), f32), shared_full, None, f32
    )
    chain = chain_dp(grad_shared)
    shared_chain = chain

    xe_own, xe_far = dispatch(h2)
    gate_grads, expert_chains, outs_own, outs_far = [], [], [], []
    for s in range(half):
        chain.advance()
        gates = after(
            jnp.concatenate([gate_own[s : s + 1], gate_far[s : s + 1]], axis=1), *chain.sent, h2_grad
        )
        outs, backs, grad, gate_grad = ffn(
            [xe_own, xe_far], [go_own, go_far], gates, expert_full[s // per_gather], s, bf16
        )
        chain.rest()
        chain = Chain(grad)
        expert_chains.append(chain)
        gate_grads.append(gate_grad)
        outs_own.append(outs[0])
        outs_far.append(outs[1])
        hot = jnp.concatenate(
            [
                own_hot[:, s * capacity : (s + 1) * capacity],
                far_hot[:, s * capacity : (s + 1) * capacity],
            ],
            axis=1,
        )
        h2_grad = h2_grad + dot(hot, jnp.concatenate([backs[0], swap_core(backs[1])], axis=0))
    gate_grads = jnp.concatenate(gate_grads, axis=0)
    gate_grad_mine = gate_grads[:, :capacity].reshape(-1)
    gate_grad_here = swap_core(gate_grads[:, capacity:]).reshape(-1)

    h2_grad_here = sum_rows(blocks_of(h2_grad))
    gate_tokens = jnp.stack(
        [
            jnp.sum(
                jnp.where(flat_slot[:, k : k + 1] == own_ids[None, :], gate_grad_mine[None, :], 0.0)
                + jnp.where(
                    flat_slot[:, k : k + 1] == far_ids[None, :], gate_grad_here[None, :], 0.0
                ),
                axis=1,
            )
            for k in range(TOP)
        ],
        axis=1,
    )
    gates_here = sum_rows(blocks_of(gate_tokens))

    router_here = router[:local_rows]
    route_grad = gates_here * kept_mine[:local_rows]
    router_grad = jnp.sum(
        jnp.where(
            routes_mine[:local_rows, :, None] == expert_ids, route_grad[:, :, None], 0.0
        ),
        axis=1,
    )
    logit_grad = (
        router_here * (router_grad - jnp.sum(router_here * router_grad, axis=-1, keepdims=True))
    ).astype(bf16)
    grad_router = dot_tn(normed_two, logit_grad)
    h2_grad_here = h2_grad_here + dot(logit_grad, router_full)
    middle_norm_grad, grad_gain_two = norm_back(middle, gain_two, h2_grad_here)
    middle_grad = out_grad.astype(f32) + middle_norm_grad
    chain.advance()
    attn_grad = gather_rows(after(middle_grad.astype(bf16), *chain.sent))

    h1_parts = [None] * peers
    query_grads = [None] * peers
    so_far = None
    for k in range(peers):
        query_grads[k], part, dkv, dkr = attend_back(
            attn_grad[k],
            q_nope,
            q_rope,
            key_rope,
            key_value,
            places[:, None],
            limit[None, :],
            cos_wide,
            sin_wide,
            weight_front,
            so_far,
            k,
            query_scale,
            bf16 if k else f32,
        )
        so_far = (dkv, dkr)
        h1_parts[k] = send_back(part, k)
    chain.rest()
    out_chain = chain_dp(outer(attended, attn_grad, d_rows))
    kv_grad, compressed_grad, grad_gain_latent = latent_back(
        dkv, dkr, compressed, cos_wide, sin_wide, gain_latent, weight_front, at_up, chunks, up_rows
    )
    compressed_round = sum_rows(blocks_of(compressed_grad)).astype(bf16)[:, :kv_cols]
    up_grad = outer([latent], [kv_grad], d_rows).reshape(chunks, dp_count, up_rows, d_rows)
    up_grad = jnp.swapaxes(up_grad, 0, 1).reshape(dp_count, chunks * up_rows, d_rows)
    query_grad = outer(query_grads, blocks_of(normed_all), d_rows)
    front_chain = chain_dp(jnp.concatenate([query_grad, up_grad], axis=1))
    normed_one = normed_all[:local_rows]
    grad_kvdown = dot_tn(normed_one, compressed_round)
    down_full = jnp.swapaxes(weight_front[:, at_kv:at_router, :], 0, 1).reshape(kv_cols, D)
    h1_grad = sum(part.astype(f32) for part in h1_parts) + dot(compressed_round, down_full)
    input_norm_grad, grad_gain_one = norm_back(x_here, gain_one, h1_grad)
    input_grad = middle_grad + input_norm_grad

    out_here = swap_core(jnp.concatenate(outs_far, axis=0))
    ffn_part = ffn_part + dot(own_hot, jnp.concatenate(outs_own, axis=0)) + dot(far_hot, out_here)
    output = (middle + sum_rows(blocks_of(ffn_part))).astype(bf16)

    gain_latent_cols = jnp.pad(
        grad_gain_latent.reshape(-1, kv_gain.shape[0]),
        ((0, 0), (0, small_rows - kv_gain.shape[0])),
    ).reshape(-1)
    small_grad = jnp.concatenate(
        [
            grad_kvdown,
            grad_router,
            grad_gain_one[:, None],
            grad_gain_two[:, None],
            gain_latent_cols[:, None],
        ],
        axis=1,
    )
    small_grad = jnp.pad(small_grad, ((0, 0), (0, -small_grad.shape[1] % 128)))
    by_peer = small_grad.reshape(dp_count, peers, small_rows, small_grad.shape[1])
    small_sum = sum_rows(
        [
            lax.dynamic_index_in_dim(by_peer, me ^ k, 1, False).reshape(
                dp_count * small_rows, small_grad.shape[1]
            )
            for k in range(peers)
        ]
    )
    small_sum = chain_dp(small_sum.astype(bf16).reshape(dp_count, small_rows, -1)).result()
    kv_out = small_sum[:, :kv_cols]
    router_out = small_sum[:, kv_cols : kv_cols + experts]
    gain_one_out = small_sum[:, kv_cols + experts]
    gain_two_out = small_sum[:, kv_cols + experts + 1]
    gain_latent_out = small_sum[: kv_gain.shape[0], kv_cols + experts + 2]

    shared_sum = shared_chain.result()
    out_sum = out_chain.result()
    front_sum = front_chain.result()
    nope_rows = heads * NOPE
    query_sum = jnp.concatenate(
        [
            front_sum[:nope_rows].reshape(heads, NOPE, d_rows),
            front_sum[nope_rows:q_cols].reshape(heads, ROPE, d_rows),
        ],
        axis=1,
    )
    query_sum = query_sum.reshape(q_cols, d_rows).T
    kvup_sum = jnp.swapaxes(front_sum[q_cols:].reshape(chunks, up_rows, d_rows), 0, 1).reshape(
        up_rows, chunks * d_rows
    )
    expert_sums = [c.result().astype(bf16) for c in expert_chains]

    mine = [lax.dynamic_index_in_dim(e, core, 0, False) for e in expert_sums]
    theirs = [swap_core(lax.dynamic_index_in_dim(e, 1 - core, 0, False)) for e in expert_sums]
    expert_grad = jnp.stack(
        [jnp.where(first, a, b) for a, b in zip(mine, theirs)]
        + [jnp.where(first, b, a) for a, b in zip(mine, theirs)],
        axis=0,
    ).astype(f32)

    return (
        output,
        input_grad,
        gain_one_out,
        query_sum,
        kv_out,
        gain_latent_out,
        kvup_sum,
        out_sum,
        gain_two_out,
        router_out,
        shared_sum[:s_cols].T,
        shared_sum[s_cols : 2 * s_cols].T,
        shared_sum[2 * s_cols :],
        jnp.swapaxes(expert_grad[:, :e_cols], 1, 2),
        jnp.swapaxes(expert_grad[:, e_cols : 2 * e_cols], 1, 2),
        expert_grad[:, 2 * e_cols :],
    )


def solution(mesh):
    placed = (
        P(("dp", "tensor"), None),
        P(("dp", "tensor"), None),
        P("dp", None),
        P("dp"),
        P("dp", None),
        P(("dp", "tensor")),
        P("dp", "tensor"),
        P(("dp", "tensor"), None),
        P(("dp", "tensor")),
        P("dp", "tensor"),
        P("tensor", "dp"),
        P(("dp", "tensor")),
        P(("dp", "tensor"), None),
        P("dp", "tensor"),
        P("dp", "tensor"),
        P("tensor", "dp"),
        P(None, "dp", "tensor"),
        P(None, "dp", "tensor"),
        P(None, "tensor", "dp"),
    )
    return jax.shard_map(
        on_device,
        mesh=mesh,
        in_specs=placed,
        out_specs=(
            P(("dp", "tensor"), None),
            P(("dp", "tensor"), None),
            P(("dp", "tensor")),
            P("dp", "tensor"),
            P(("dp", "tensor"), None),
            P(("dp", "tensor")),
            P("dp", "tensor"),
            P("tensor", "dp"),
            P(("dp", "tensor")),
            P(("dp", "tensor"), None),
            P("dp", "tensor"),
            P("dp", "tensor"),
            P("tensor", "dp"),
            P(None, "dp", "tensor"),
            P(None, "dp", "tensor"),
            P(None, "tensor", "dp"),
        ),
        check_vma=False,
    )
```

```python
import functools

import jax
import jax.numpy as jnp
from jax import lax
from jax.experimental import pallas as pl
from jax.experimental.pallas import tpu as pltpu
from jax.sharding import PartitionSpec as P

D = 2048
NOPE = 128
ROPE = 64
VD = 128
KVR = 512
TOP = 2
LENGTH = 1024

eps = 1e-06
bf16 = jnp.bfloat16
f32 = jnp.float32


def dot(a, b, dims=((1,), (0,)), out=f32):
    return lax.dot_general(a, b, (dims, ((), ())), preferred_element_type=f32).astype(out)


def dot_nt(a, b, out=f32):
    return dot(a, b, ((1,), (1,)), out)


def dot_tn(a, b, out=f32):
    return dot(a, b, ((0,), (0,)), out)


def inv_rms(values):
    return lax.rsqrt(jnp.mean(values * values, axis=-1, keepdims=True) + eps)


def norm_rows(values, gain_vec):
    return values * inv_rms(values) * gain_vec


def norm_back(values, gain_vec, upstream):
    inv = inv_rms(values)
    scaled = upstream * gain_vec
    grad = inv * scaled - values * (
        inv * inv * inv * jnp.mean(values * scaled, axis=-1, keepdims=True)
    )
    return grad, jnp.sum(upstream * values * inv, axis=0)


def swap_core(values):
    count = lax.axis_size("dp")
    return lax.ppermute(values, "dp", [(i, i ^ 1) for i in range(count)])


def gather_rows(values):
    count = lax.axis_size("tensor")
    return [values] + [
        lax.ppermute(values, "tensor", [(i, i ^ k) for i in range(count)])
        for k in range(count - 1, 0, -1)
    ][::-1]


def send_back(part, k):
    count = lax.axis_size("tensor")
    return part if k == 0 else lax.ppermute(part, "tensor", [(i, i ^ k) for i in range(count)])


def sum_rows(blocks):
    count = lax.axis_size("tensor")
    total = blocks[0].astype(f32)
    arrived = [
        lax.ppermute(blocks[k].astype(bf16), "tensor", [(i, i ^ k) for i in range(count)])
        for k in range(count - 1, 0, -1)
    ]
    for piece in arrived:
        total = total + piece.astype(f32)
    return total


NT=(((1,),(1,)),((),())); NN=(((1,),(0,)),((),()))
def mm(a,b,dims=NN): return lax.dot_general(a,b,dims,preferred_element_type=f32)

def ffn_kernel(parts, hidden_cols, *refs):
    x_refs=refs[:parts]; g_refs=refs[parts:2*parts]; gate_ref, w_ref = refs[2*parts:2*parts+2]
    outs=refs[2*parts+2:]
    out_refs=outs[:parts]; back_refs=outs[parts:2*parts]; grad_ref, dgate_ref = outs[2*parts:2*parts+2]
    val, raw, back_t, gated_t, back_n, gated_n = outs[2*parts+2:]
    phase=pl.program_id(0); step=pl.program_id(1)
    F=hidden_cols
    def rows_of(rs):
        pieces=[r[...].reshape(r.shape[-2:]) for r in rs]
        return pieces[0] if parts==1 else jnp.concatenate(pieces,axis=0)
    x=rows_of(x_refs); g=rows_of(g_refs)
    w=w_ref[...].reshape(w_ref.shape[-2:])
    @pl.when(phase==0)
    def _():
        a=mm(w[:2*F],x,NT); b=mm(w[2*F:],g,NT)
        @pl.when(step==0)
        def _():
            val[...]=a; raw[...]=b
        @pl.when(step>0)
        def _():
            val[...]+=a; raw[...]+=b
    @pl.when((phase==1)&(step==0))
    def _():
        eg=val[:F]; eu=val[F:]; r=raw[...]; gate=gate_ref[...]
        s=jax.nn.sigmoid(eg); act=eg*s
        hid=(act*eu).astype(bf16).astype(f32)
        dgate_ref[...]=jnp.sum(hid*r,axis=0,keepdims=True)
        gated=(hid*gate).astype(bf16)
        d=r*gate
        bg=(d*eu*s*(1.0+eg*(1.0-s))).astype(bf16); bu=(d*act).astype(bf16)
        back_t[:F]=bg; back_t[F:]=bu; gated_t[...]=gated
        back_n[...]=back_t[...].T; gated_n[...]=gated.T
    @pl.when(phase==1)
    def _():
        o=mm(gated_n[...],w[2*F:]); b=mm(back_n[...],w[:2*F])
        at=0
        for ro,rb in zip(out_refs,back_refs):
            n=ro.shape[-2]
            ro[...]=o[at:at+n].astype(ro.dtype).reshape(ro.shape); rb[...]=b[at:at+n].astype(rb.dtype).reshape(rb.shape); at+=n
        sh=grad_ref.shape[:-2]
        gr=jnp.concatenate([mm(back_t[...],x),mm(gated_t[...],g)],axis=0).astype(bf16)
        grad_ref[...]=gr.reshape(grad_ref.shape)

def ffn(xs, gs, gates, w, stage, out_dtype):
    parts=len(xs)
    F=w.shape[-2]//3; dl=w.shape[-1]
    D=xs[0].shape[-1]; nd=D//dl
    ns=[x.shape[-2] for x in xs]; n=sum(ns)
    if stage is None:
        row_spec=[pl.BlockSpec((m,dl),lambda p,j:(0,j)) for m in ns]
        w_spec=pl.BlockSpec((1,3*F,dl),lambda p,j:(j,0,0))
        g_shape=(nd,3*F,dl); g_spec=pl.BlockSpec((1,3*F,dl),lambda p,j:(j*p,0,0))
    else:
        row_spec=[pl.BlockSpec((1,m,dl),lambda p,j:(stage,0,j)) for m in ns]
        ws=stage%w.shape[1]
        w_spec=pl.BlockSpec((1,1,1,3*F,dl),lambda p,j:(j//2,ws,j%2,0,0))
        g_shape=(nd//2,2,3*F,dl); g_spec=pl.BlockSpec((1,1,3*F,dl),lambda p,j:((j*p)//2,(j*p)%2,0,0))
    out_spec=[pl.BlockSpec((m,dl),lambda p,j:(0,j*p)) for m in ns]
    flops=2*n*D*F*9
    res = pl.pallas_call(
        functools.partial(ffn_kernel,parts,F),
        grid=(2,nd),
        in_specs=row_spec*2+[pl.BlockSpec((1,n),lambda p,j:(0,0)),w_spec],
        out_specs=out_spec*2+[g_spec,pl.BlockSpec((1,n),lambda p,j:(0,0))],
        out_shape=[jax.ShapeDtypeStruct((m,D),out_dtype) for m in ns]*2+[jax.ShapeDtypeStruct(g_shape,bf16),jax.ShapeDtypeStruct((1,n),f32)],
        scratch_shapes=[pltpu.VMEM((2*F,n),f32),pltpu.VMEM((F,n),f32),pltpu.VMEM((2*F,n),bf16),pltpu.VMEM((F,n),bf16),pltpu.VMEM((n,2*F),bf16),pltpu.VMEM((n,F),bf16)],
        compiler_params=pltpu.CompilerParams(dimension_semantics=("arbitrary","arbitrary"),vmem_limit_bytes=60*1024*1024),
        cost_estimate=pl.CostEstimate(flops=flops,bytes_accessed=2*3*F*D*3+2*n*D*6,transcendentals=n*F),
        name="ffn",
    )(*xs,*gs,gates,w)
    return res[:parts], res[parts:2*parts], res[2*parts], res[2*parts+1]


def front_kernel(sizes, x_ref, w_ref, cos_ref, sin_ref, gl_ref, h_ref, qn_ref, qr_ref, comp_ref, lat_ref, kr_ref, kv_ref, extra, ups):
    heads, at_q, at_kv, at_gain, at_up, chunks, up_rows, scale = sizes
    nd, _, dl = w_ref.shape
    qn_cols, qr_cols = heads * NOPE, heads * ROPE
    half = ROPE // 2
    main = qn_cols + qr_cols + KVR

    @pl.when(pl.program_id(0) == 0)
    def _():
        for j in range(nd):
            w_r = w_ref[j, at_q + qn_cols : at_q + qn_cols + qr_cols, :]
            w_k = w_ref[j, at_kv + KVR : at_kv + KVR + ROPE, :]
            swapped = []
            for h in range(heads):
                swapped.append(w_r[h * ROPE + half : (h + 1) * ROPE])
                swapped.append(w_r[h * ROPE : h * ROPE + half])
            extra[j] = jnp.concatenate(
                swapped + [w_k, w_k, w_k[half:], w_k[:half], w_k[half:], w_k[:half]], axis=0
            )
            for c in range(chunks):
                at = at_up + c * up_rows
                ups[c, j * up_rows : (j + 1) * up_rows, :] = w_ref[j, at : at + up_rows, :]

    x = x_ref[...].astype(f32)
    inv = lax.rsqrt(jnp.mean(x * x, axis=-1, keepdims=True) + eps)
    acc = None
    for j in range(nd):
        gain = w_ref[j, at_gain : at_gain + 16, :][0:1].astype(f32)
        h = (x[:, j * dl : (j + 1) * dl] * inv * gain).astype(bf16)
        h_ref[:, j * dl : (j + 1) * dl] = h
        part = [mm(h, w_ref[j, at_q : at_q + main, :], NT), mm(h, extra[j], NT)]
        acc = part if acc is None else [a + b for a, b in zip(acc, part)]
    a, b = acc
    cos, sin = cos_ref[...], sin_ref[...]
    qn_ref[...] = (a[:, :qn_cols] * scale).astype(bf16)
    qr_ref[...] = (
        (a[:, qn_cols : qn_cols + qr_cols] * cos + b[:, :qr_cols] * sin) * scale
    ).astype(bf16)
    comp = a[:, qn_cols + qr_cols :]
    comp_ref[...] = comp
    wide = 2 * ROPE
    kr_ref[...] = (
        b[:, qr_cols : qr_cols + wide] * cos[:, :wide]
        + b[:, qr_cols + wide : qr_cols + 2 * wide] * sin[:, :wide]
    ).astype(bf16)
    lat = (
        comp * lax.rsqrt(jnp.mean(comp * comp, axis=-1, keepdims=True) + eps) * gl_ref[...]
    ).astype(bf16)
    lat_ref[...] = lat
    for c in range(chunks):
        kv_ref[:, c * dl : (c + 1) * dl] = mm(lat, ups[c]).astype(bf16)


def front(x, w, cos, sin, gain_latent, sizes):
    heads, at_q, at_kv, at_gain, at_up, chunks, up_rows, scale = sizes
    rows, width = x.shape
    nd, _, dl = w.shape
    tb = min(256, rows)
    row = lambda cols: pl.BlockSpec((tb, cols), lambda i: (i, 0))
    whole = lambda a: pl.BlockSpec(a.shape, lambda i: (0,) * a.ndim)
    cols = [width, heads * NOPE, heads * ROPE, KVR, KVR, 2 * ROPE, heads * (NOPE + VD)]
    kinds = [bf16, bf16, bf16, f32, bf16, bf16, bf16]
    return pl.pallas_call(
        functools.partial(front_kernel, sizes),
        grid=(rows // tb,),
        in_specs=[row(width), whole(w), row(heads * ROPE), row(heads * ROPE), whole(gain_latent)],
        out_specs=[row(c) for c in cols],
        out_shape=[jax.ShapeDtypeStruct((rows, c), k) for c, k in zip(cols, kinds)],
        scratch_shapes=[
            pltpu.VMEM((nd, heads * ROPE + 4 * ROPE, dl), bf16),
            pltpu.VMEM((chunks, nd * up_rows, dl), bf16),
        ],
        compiler_params=pltpu.CompilerParams(vmem_limit_bytes=60 * 1024 * 1024),
        cost_estimate=pl.CostEstimate(
            flops=2 * rows * width * 1900, bytes_accessed=2 * w.size + 12 * rows * width, transcendentals=0
        ),
        name="front",
    )(x, w, cos, sin, gain_latent)


def head_rope(wide, h):
    lane = lax.broadcasted_iota(jnp.int32, wide.shape, 1)
    return jnp.where((lane // ROPE) == (h % 2), wide, jnp.zeros_like(wide))


def attend_kernel(heads, qn_ref, qr_ref, kr_ref, kv_ref, kpos_ref, lim_ref, w_ref, att_ref, out_ref):
    kr = kr_ref[...]
    keep = kpos_ref[...] <= lim_ref[...]
    wide = 2 * ROPE
    for h in range(heads):
        at = h * (NOPE + VD)
        q = jnp.concatenate(
            [
                qn_ref[:, h * NOPE : (h + 1) * NOPE],
                head_rope(qr_ref[:, (h // 2) * wide : (h // 2 + 1) * wide], h),
            ],
            axis=1,
        )
        k = jnp.concatenate([kv_ref[:, at : at + NOPE], kr], axis=1)
        s = jnp.where(keep, mm(q, k, NT), -1e30)
        p = jnp.exp(s - jnp.max(s, axis=1, keepdims=True))
        p = (p * (1.0 / jnp.sum(p, axis=1, keepdims=True))).astype(bf16)
        att_ref[:, h * VD : (h + 1) * VD] = mm(p, kv_ref[:, at + NOPE : at + NOPE + VD]).astype(bf16)
    att = att_ref[...]
    dl = w_ref.shape[2]
    for j in range(w_ref.shape[0]):
        out_ref[:, j * dl : (j + 1) * dl] = mm(att, w_ref[j]).astype(out_ref.dtype)


def attend(qn, qr, kr, kv, kpos, limit, w, block, block_rows, out_dtype):
    rows = qn.shape[0]
    heads = qn.shape[1] // NOPE
    nd, _, dl = w.shape
    row = lambda cols: pl.BlockSpec((block_rows, cols), lambda i: (block, 0))
    whole = lambda a: pl.BlockSpec(a.shape, lambda i: (0,) * a.ndim)
    first = lambda cols: pl.BlockSpec((block_rows, cols), lambda i: (0, 0))
    return pl.pallas_call(
        functools.partial(attend_kernel, heads),
        grid=(1,),
        in_specs=[
            row(heads * NOPE),
            row(heads * ROPE),
            whole(kr),
            whole(kv),
            whole(kpos),
            row(1),
            pl.BlockSpec((nd, heads * VD, dl), lambda i: (0, 0, 0)),
        ],
        out_specs=[first(heads * VD), first(nd * dl)],
        out_shape=[
            jax.ShapeDtypeStruct((block_rows, heads * VD), bf16),
            jax.ShapeDtypeStruct((block_rows, nd * dl), out_dtype),
        ],
        compiler_params=pltpu.CompilerParams(vmem_limit_bytes=60 * 1024 * 1024),
        cost_estimate=pl.CostEstimate(
            flops=2 * block_rows * heads * (rows * 384 + VD * nd * dl),
            bytes_accessed=8 * 1024 * 1024,
            transcendentals=block_rows * heads * rows,
        ),
        name="attend",
    )(qn, qr, kr, kv, kpos, limit, w)


def rot_back(v, cos, sin):
    half = ROPE // 2
    lane = lax.broadcasted_iota(jnp.int32, v.shape, 1)
    width = v.shape[1]
    down = pltpu.roll(v, width - half, 1)
    up = pltpu.roll(v, half, 1)
    other = jnp.where(lane % ROPE < half, down, up)
    return v * cos - other * sin


def attend_back_kernel(heads, scale, first, *refs):
    da_ref, qn_ref, qr_ref, kr_ref, kv_ref, kpos_ref, lim_ref, cos_ref, sin_ref = refs[:9]
    wo_ref, wa_ref, wb_ref, wr_ref = refs[9:13]
    dkv_in, dkr_in = (None, None) if first else refs[13:15]
    dq_ref, dh_ref, dkv_ref, dkr_ref = refs[13 if first else 15 :]
    nd, _, dl = wo_ref.shape
    wide = 2 * ROPE
    width = NOPE + VD
    grad = None
    for j in range(nd):
        part = mm(da_ref[:, j * dl : (j + 1) * dl], wo_ref[j], NT)
        grad = part if grad is None else grad + part
    grad = grad.astype(bf16)
    kr = kr_ref[...]
    keep = kpos_ref[...] <= lim_ref[...]
    rope_grads = []
    dkr = jnp.zeros(dkr_ref.shape, f32) if first else dkr_in[...]
    for h in range(heads):
        at = h * width
        q = jnp.concatenate(
            [
                qn_ref[:, h * NOPE : (h + 1) * NOPE],
                head_rope(qr_ref[:, (h // 2) * wide : (h // 2 + 1) * wide], h),
            ],
            axis=1,
        )
        k = jnp.concatenate([kv_ref[:, at : at + NOPE], kr], axis=1)
        do = grad[:, h * VD : (h + 1) * VD]
        s = jnp.where(keep, mm(k, q, NT), -1e30)
        p = jnp.exp(s - jnp.max(s, axis=0, keepdims=True))
        p = p * (1.0 / jnp.sum(p, axis=0, keepdims=True))
        dp = mm(kv_ref[:, at + NOPE : at + width], do, NT)
        ds = (p * (dp - jnp.sum(p * dp, axis=0, keepdims=True))).astype(bf16)
        dv = mm(p.astype(bf16), do)
        dk = mm(ds, q)
        if first:
            dkv_ref[:, at : at + NOPE] = dk[:, :NOPE]
            dkv_ref[:, at + NOPE : at + width] = dv
        else:
            dkv_ref[:, at : at + NOPE] = dkv_in[:, at : at + NOPE] + dk[:, :NOPE]
            dkv_ref[:, at + NOPE : at + width] = dkv_in[:, at + NOPE : at + width] + dv
        dkr = dkr + dk[:, NOPE:]
        dq = lax.dot_general(ds, k, (((0,), (0,)), ((), ())), preferred_element_type=f32)
        dq_ref[:, h * NOPE : (h + 1) * NOPE] = (dq[:, :NOPE] * scale).astype(bf16)
        masked = head_rope(dq[:, NOPE:], h)
        if h % 2:
            rope_grads[-1] = rope_grads[-1] + masked
        else:
            rope_grads.append(masked)
    dkr_ref[...] = dkr
    ropes = rope_grads[0] if len(rope_grads) == 1 else jnp.concatenate(rope_grads, axis=1)
    at = heads * NOPE
    dq_ref[:, at:] = (rot_back(ropes, cos_ref[...], sin_ref[...]) * scale).astype(bf16)
    half = at // 2
    for j in range(nd):
        dh_ref[:, j * dl : (j + 1) * dl] = (
            mm(dq_ref[:, :half], wa_ref[j])
            + mm(dq_ref[:, half:at], wb_ref[j])
            + mm(dq_ref[:, at:], wr_ref[j])
        ).astype(dh_ref.dtype)


def attend_back(da, qn, qr, kr, kv, kpos, limit, cos, sin, w, so_far, block, scale, out_dtype):
    block_rows = da.shape[0]
    rows = qn.shape[0]
    heads = qn.shape[1] // NOPE
    nd, _, dl = w.shape
    row = lambda cols: pl.BlockSpec((block_rows, cols), lambda i: (block, 0))
    whole = lambda a: pl.BlockSpec(a.shape, lambda i: (0,) * a.ndim)
    rows_w = lambda size, at: pl.BlockSpec((nd, size, dl), lambda i: (0, at, 0))
    part = heads * ROPE
    dkv = jax.ShapeDtypeStruct((rows, heads * (NOPE + VD)), f32)
    dkr = jax.ShapeDtypeStruct((rows, 2 * ROPE), f32)
    first = so_far is None
    return pl.pallas_call(
        functools.partial(attend_back_kernel, heads, scale, first),
        grid=(1,),
        in_specs=[
            whole(da),
            row(heads * NOPE),
            row(heads * ROPE),
            whole(kr),
            whole(kv),
            whole(kpos),
            pl.BlockSpec((1, block_rows), lambda i: (0, block)),
            row(heads * ROPE),
            row(heads * ROPE),
            rows_w(2 * part, 0),
            rows_w(part, 2),
            rows_w(part, 3),
            rows_w(part, 4),
        ]
        + ([] if first else [whole(dkv), whole(dkr)]),
        out_specs=[
            pl.BlockSpec((block_rows, 3 * part), lambda i: (0, 0)),
            pl.BlockSpec((block_rows, nd * dl), lambda i: (0, 0)),
            whole(dkv),
            whole(dkr),
        ],
        out_shape=[
            jax.ShapeDtypeStruct((block_rows, 3 * part), bf16),
            jax.ShapeDtypeStruct((block_rows, nd * dl), out_dtype),
            dkv,
            dkr,
        ],
        input_output_aliases={} if first else {13: 2, 14: 3},
        compiler_params=pltpu.CompilerParams(vmem_limit_bytes=60 * 1024 * 1024),
        cost_estimate=pl.CostEstimate(
            flops=2 * block_rows * heads * (rows * 1024 + 5 * ROPE * nd * dl),
            bytes_accessed=20 * 1024 * 1024,
            transcendentals=block_rows * heads * rows,
        ),
        name="attend_back",
    )(da, qn, qr, kr, kv, kpos, limit, cos, sin, w, w, w, w, *(() if first else so_far))


def latent_back_kernel(sizes, dkv_ref, dkr_ref, comp_ref, cos_ref, sin_ref, gl_ref, w_ref, dkvb_ref, dc_ref, dg_ref, ups):
    chunks, up_rows, in_rows = sizes
    nd, _, dl = w_ref.shape
    dkv = dkv_ref[...].astype(bf16)
    dkvb_ref[...] = dkv

    @pl.when(pl.program_id(0) == 0)
    def _():
        for j in range(nd):
            for c in range(chunks):
                at = in_rows + c * up_rows
                ups[c, j * up_rows : (j + 1) * up_rows, :] = w_ref[j, at : at + up_rows, :]

    dlat = None
    for c in range(chunks):
        part = mm(dkv[:, c * dl : (c + 1) * dl], ups[c], NT)
        dlat = part if dlat is None else dlat + part
    comp = comp_ref[...]
    inv = lax.rsqrt(jnp.mean(comp * comp, axis=-1, keepdims=True) + eps)
    scaled = dlat * gl_ref[...]
    dc_ref[:, :KVR] = (
        inv * scaled - comp * (inv * inv * inv * jnp.mean(comp * scaled, axis=-1, keepdims=True))
    ).astype(dc_ref.dtype)
    dg = jnp.sum(dlat * comp * inv, axis=0, keepdims=True)

    @pl.when(pl.program_id(0) == 0)
    def _():
        dg_ref[...] = dg

    @pl.when(pl.program_id(0) > 0)
    def _():
        dg_ref[...] += dg

    dkr = dkr_ref[...]
    dkr = dkr + pltpu.roll(dkr, ROPE, 1)
    wide = 2 * ROPE
    dkr = rot_back(dkr, cos_ref[:, :wide], sin_ref[:, :wide])
    lane = lax.broadcasted_iota(jnp.int32, dkr.shape, 1)
    dc_ref[:, KVR:] = jnp.where(lane < ROPE, dkr, 0.0).astype(dc_ref.dtype)


def latent_back(dkv, dkr, comp, cos, sin, gain_latent, w, at_up, chunks, up_rows):
    rows = dkv.shape[0]
    nd, _, dl = w.shape
    tb = min(256, rows)
    row = lambda cols: pl.BlockSpec((tb, cols), lambda i: (i, 0))
    whole = lambda a: pl.BlockSpec(a.shape, lambda i: (0,) * a.ndim)
    return pl.pallas_call(
        functools.partial(latent_back_kernel, (chunks, up_rows, at_up)),
        grid=(rows // tb,),
        in_specs=[
            row(dkv.shape[1]),
            row(dkr.shape[1]),
            row(KVR),
            row(cos.shape[1]),
            row(cos.shape[1]),
            whole(gain_latent),
            whole(w),
        ],
        out_specs=[row(dkv.shape[1]), row(KVR + 2 * ROPE), pl.BlockSpec((1, KVR), lambda i: (0, 0))],
        out_shape=[
            jax.ShapeDtypeStruct(dkv.shape, bf16),
            jax.ShapeDtypeStruct((rows, KVR + 2 * ROPE), bf16),
            jax.ShapeDtypeStruct((1, KVR), f32),
        ],
        scratch_shapes=[pltpu.VMEM((chunks, nd * up_rows, dl), bf16)],
        compiler_params=pltpu.CompilerParams(vmem_limit_bytes=60 * 1024 * 1024),
        cost_estimate=pl.CostEstimate(
            flops=2 * rows * KVR * dkv.shape[1], bytes_accessed=16 * 1024 * 1024, transcendentals=0
        ),
        name="latent_back",
    )(dkv, dkr, comp, cos, sin, gain_latent, w)


def outer_kernel(parts, *refs):
    a_refs, b_refs, out_ref, at_ref = refs[:parts], refs[parts : 2 * parts], refs[-2], refs[-1]

    @pl.when(pl.program_id(0) == 0)
    def _():
        at = 0
        for a in a_refs:
            at_ref[:, at : at + a.shape[0]] = a[...].T
            at += a.shape[0]

    right = b_refs[0][...] if parts == 1 else jnp.concatenate([b[...] for b in b_refs], axis=0)
    out_ref[...] = mm(at_ref[...], right).astype(bf16)[None]


def outer(left, right, width):
    parts = len(left)
    rows = sum(a.shape[0] for a in left)
    cols = left[0].shape[1]
    count = right[0].shape[1] // width
    return pl.pallas_call(
        functools.partial(outer_kernel, parts),
        grid=(count,),
        in_specs=[pl.BlockSpec(a.shape, lambda j: (0, 0)) for a in left]
        + [pl.BlockSpec((b.shape[0], width), lambda j: (0, j)) for b in right],
        out_specs=pl.BlockSpec((1, cols, width), lambda j: (j, 0, 0)),
        out_shape=jax.ShapeDtypeStruct((count, cols, width), bf16),
        scratch_shapes=[pltpu.VMEM((cols, rows), bf16)],
        compiler_params=pltpu.CompilerParams(vmem_limit_bytes=60 * 1024 * 1024),
        cost_estimate=pl.CostEstimate(
            flops=2 * rows * cols * count * width,
            bytes_accessed=2 * (rows * cols + (rows + cols) * count * width),
            transcendentals=0,
        ),
        name="outer",
    )(*left, *right)


def combine_kernel(parts, *refs):
    slot_ref, acc_ref = refs[:2]
    id_refs, row_refs, out_ref = refs[2 : 2 + parts], refs[2 + parts : 2 + 2 * parts], refs[-1]
    one, two = slot_ref[:, 0:1], slot_ref[:, 1:2]
    total = acc_ref[...].astype(f32)
    for ids, rows in zip(id_refs, row_refs):
        hot = ((one == ids[...]) | (two == ids[...])).astype(f32).astype(bf16)
        total = total + mm(hot, rows[...])
    out_ref[...] = total.astype(out_ref.dtype)


def combine(acc, slots, ids, rows, block_rows, first, count, out_dtype):
    parts = len(ids)
    width = acc.shape[1]
    whole = lambda a: pl.BlockSpec(a.shape, lambda i: (0, 0))
    return pl.pallas_call(
        functools.partial(combine_kernel, parts),
        grid=(count,),
        in_specs=[
            pl.BlockSpec((block_rows, TOP), lambda i: (i + first, 0)),
            pl.BlockSpec((block_rows, width), lambda i: (i + first, 0)),
        ]
        + [whole(a) for a in ids]
        + [whole(a) for a in rows],
        out_specs=pl.BlockSpec((block_rows, width), lambda i: (i, 0)),
        out_shape=jax.ShapeDtypeStruct((count * block_rows, width), out_dtype),
        compiler_params=pltpu.CompilerParams(vmem_limit_bytes=60 * 1024 * 1024),
        cost_estimate=pl.CostEstimate(flops=1000000, bytes_accessed=1000000, transcendentals=0),
        name="combine",
    )(slots, acc, *ids, *rows)


def after(values, *others):
    return lax.optimization_barrier((values, *others))[0]


def sync(chains, *values):
    live = [c.live for c in chains]
    live, values = lax.optimization_barrier((live, values))
    for c, v in zip(chains, live):
        c.live = v
    return values


def rising_pairs(low, high):
    return [(2 * j + c, 2 * j + 2 + c) for j in range(low, high) for c in range(2)]


def falling_pairs(low, high):
    return [(2 * j + c, 2 * j - 2 + c) for j in range(low, high) for c in range(2)]


class Chain:
    def __init__(self, blocks):
        self.blocks = blocks
        self.nz = lax.axis_size("dp") // 2
        self.place = lax.axis_index("dp") // 2
        self.live = (blocks,)
        self.done = 0

    def term(self, index):
        return lax.dynamic_index_in_dim(self.blocks, jnp.clip(index, 0, self.nz - 1), 0, False)

    def advance(self):
        nz, place, step = self.nz, self.place, self.done
        if step >= nz - 1:
            return
        if step == 0:
            self.blocks = self.live[0]
        up, down = self.term(nz - 1 - step + place), self.term(step - nz + 1 + place)
        if step > 0:
            up = (up.astype(f32) + self.live[0].astype(f32)).astype(bf16)
            down = (down.astype(f32) + self.live[1].astype(f32)).astype(bf16)
        self.live = (
            lax.ppermute(up, "dp", rising_pairs(0, min(step + 1, nz - 1))),
            lax.ppermute(down, "dp", falling_pairs(max(nz - 1 - step, 1), nz)),
        )
        self.done += 1

    def rest(self):
        while self.done < self.nz - 1:
            self.advance()

    def result(self):
        self.rest()
        if self.nz == 1:
            return self.blocks[0].astype(f32)
        return self.term(self.place).astype(f32) + self.live[0].astype(f32) + self.live[1].astype(f32)


class Gather:
    def __init__(self, block):
        self.block = block
        self.nz = lax.axis_size("dp") // 2
        self.place = lax.axis_index("dp") // 2
        self.live = (block, block)
        self.arrived = []
        self.done = 0

    def advance(self):
        nz, step = self.nz, self.done
        if step >= nz - 1:
            return
        if step > 0:
            self.arrived.append(self.live)
        self.live = (
            lax.ppermute(self.live[0], "dp", rising_pairs(step, nz - 1)),
            lax.ppermute(self.live[1], "dp", falling_pairs(1, nz - step)),
        )
        self.done += 1

    def rest(self):
        while self.done < self.nz - 1:
            self.advance()

    def result(self):
        self.rest()
        arrived = self.arrived + ([self.live] if self.nz > 1 else [])
        full = jnp.zeros((self.nz, *self.block.shape), self.block.dtype)
        put = lambda full, block, at: lax.dynamic_update_index_in_dim(
            full, block, jnp.clip(at, 0, self.nz - 1), 0
        )
        for step in range(len(arrived) - 1, -1, -1):
            full = put(full, arrived[step][0], self.place - 1 - step)
        for step in range(len(arrived) - 1, -1, -1):
            full = put(full, arrived[step][1], self.place + 1 + step)
        return put(full, self.block, self.place)


class Flow:
    def __init__(self):
        self.active = []

    def add(self, *items):
        self.active += items

    def start(self, item):
        item.advance()
        self.add(item)

    def tick(self, *values):
        values = sync(self.active, *values)
        self.active = [c for c in self.active if c.done < c.nz - 1]
        for c in self.active:
            c.advance()
        return values


def pair_sums(grad):
    count = lax.axis_size("dp")
    core = lax.axis_index("dp") % 2
    parts = grad.reshape(count // 2, 2, grad.shape[1], grad.shape[2])
    other = lax.dynamic_index_in_dim(parts, 1 - core, 1, False)
    mine = lax.dynamic_index_in_dim(parts, core, 1, False)
    return (mine.astype(f32) + swap_core(other).astype(f32)).astype(bf16)


def chain_dp(grad):
    chain = Chain(pair_sums(grad))
    chain.advance()
    return chain


def on_device(
    block_input,
    out_grad,
    routes,
    prefixes,
    drop_order,
    attn_gain,
    query_proj,
    kv_down,
    kv_gain,
    kv_up,
    out_proj,
    ffn_gain,
    router_proj,
    shared_gate,
    shared_up,
    shared_down,
    expert_gate,
    expert_up,
    expert_down,
):
    me = lax.axis_index("tensor")
    place = lax.axis_index("dp")
    core = place % 2
    peers = lax.axis_size("tensor")
    dp_count = lax.axis_size("dp")
    nz = dp_count // 2
    local_rows = block_input.shape[0]
    rows = routes.shape[0]
    experts = expert_gate.shape[0]
    half = experts // 2
    capacity = rows * TOP * 9 // (8 * experts)
    qk_width = NOPE + ROPE
    query_scale = qk_width ** (-0.5)
    q_cols = query_proj.shape[1]
    heads = q_cols // qk_width
    d_rows = query_proj.shape[0]
    s_cols = shared_gate.shape[1]
    e_cols = expert_gate.shape[2]

    def in_order(array):
        return jnp.concatenate(
            [
                lax.dynamic_slice_in_dim(array, (me ^ k) * local_rows, local_rows, 0)
                for k in range(peers)
            ],
            axis=0,
        )

    small_rows = kv_down.shape[0]

    def column(vector):
        return jnp.pad(vector, (0, small_rows - vector.shape[0]))[:, None]

    small = jnp.concatenate(
        [kv_down, router_proj, column(attn_gain), column(ffn_gain), column(kv_gain)], axis=1
    )
    kv_cols = kv_down.shape[1]
    small_count = small.shape[1] + (-small.shape[1] % 16)
    small = jnp.pad(small, ((0, 0), (0, -small.shape[1] % 128)))
    small_blocks = gather_rows(small)
    x_blocks = gather_rows(block_input)
    go_blocks = gather_rows(out_grad)
    x_all = jnp.concatenate(x_blocks, axis=0)

    small_all = jnp.zeros((peers * small_rows, small.shape[1]), bf16)
    for k, block in enumerate(small_blocks):
        small_all = lax.dynamic_update_slice_in_dim(small_all, block, (me ^ k) * small_rows, 0)
    by_head = query_proj.reshape(d_rows, heads, qk_width)
    up_rows = kv_up.shape[0]
    chunks_up = kv_up.shape[1] // d_rows
    front_local = jnp.concatenate(
        [
            out_proj,
            by_head[:, :, :NOPE].reshape(d_rows, heads * NOPE).T,
            by_head[:, :, NOPE:].reshape(d_rows, heads * ROPE).T,
            small_all[:, :small_count].T,
            jnp.swapaxes(kv_up.reshape(up_rows, chunks_up, d_rows), 0, 1).reshape(-1, d_rows),
        ],
        axis=0,
    )
    at_q = heads * VD
    at_kv = at_q + q_cols
    at_router = at_kv + kv_cols
    at_gain = at_router + experts
    at_up = at_kv + small_count
    weight_front = lax.all_gather(front_local, "dp", axis=0)
    router_full = jnp.swapaxes(weight_front[:, at_router:at_gain, :], 0, 1).reshape(experts, D)
    gain_one = weight_front[:, at_gain, :].reshape(1, D).astype(f32)
    gain_two = weight_front[:, at_gain + 1, :].reshape(1, D).astype(f32)
    gain_latent = (
        weight_front[:, at_gain + 2, :]
        .reshape(-1, small_rows)[:, : kv_gain.shape[0]]
        .reshape(1, KVR)
        .astype(f32)
    )
    shared_local = jnp.concatenate([shared_gate.T, shared_up.T, shared_down], axis=0)
    shared_full = lax.all_gather(shared_local, "dp", axis=0)

    expert_local = jnp.concatenate(
        [jnp.swapaxes(expert_gate, 1, 2), jnp.swapaxes(expert_up, 1, 2), expert_down], axis=1
    )
    kept_part = lax.dynamic_slice_in_dim(expert_local, core * half, half, 0)
    sent_part = lax.dynamic_slice_in_dim(expert_local, (1 - core) * half, half, 0)
    got_part = swap_core(sent_part)
    first = core == 0
    pair_part = jnp.stack(
        [jnp.where(first, kept_part, got_part), jnp.where(first, got_part, kept_part)], axis=1
    ).reshape(half * 2 * 3 * e_cols, d_rows)
    groups = [[2 * j + c for j in range(nz)] for c in range(2)]
    size = 2 * 3 * e_cols
    pieces = [pair_part[s * size : (s + 1) * size] for s in range(half)]
    expert_full = [
        lax.all_gather(pieces[0], "dp", axis=0, tiled=True, axis_index_groups=groups).reshape(
            nz, 1, 2, 3 * e_cols, d_rows
        )
    ]

    token_ids = jnp.arange(rows, dtype=jnp.int32)
    ranking = jnp.sum(
        jnp.where(drop_order[0][:, None] == token_ids[None, :], token_ids[:, None], 0), axis=0
    )
    expert_ids = jnp.arange(experts, dtype=jnp.int32)
    chosen = jnp.sum((routes[:, :, None] == expert_ids).astype(f32), axis=1)
    earlier = (ranking[None, :] < ranking[:, None]).astype(bf16)
    before = dot(earlier, chosen.astype(bf16)).astype(jnp.int32)
    slot_rank = jnp.sum(
        jnp.where(routes[:, :, None] == expert_ids, before[:, None, :], 0), axis=2
    )
    kept_mask = slot_rank < capacity
    flat_slot = in_order(jnp.where(kept_mask, routes * capacity + slot_rank, -1))
    routes_mine = in_order(routes)
    kept_mine = (flat_slot >= 0).astype(f32)
    slots = half * capacity
    slot_ids = jnp.arange(slots, dtype=jnp.int32)
    own_ids = core * slots + slot_ids
    far_ids = (1 - core) * slots + slot_ids

    def one_hot(ids):
        return (
            (flat_slot[:, 0:1] == ids[None, :]) | (flat_slot[:, 1:2] == ids[None, :])
        ).astype(bf16)

    own_hot = one_hot(own_ids)
    far_hot = one_hot(far_ids)

    def dispatch(values):
        return (
            dot_tn(own_hot, values, bf16).reshape(half, capacity, D),
            swap_core(dot_tn(far_hot, values, bf16)).reshape(half, capacity, D),
        )


    places = in_order(token_ids)
    half_width = ROPE // 2
    frequency = jnp.exp(
        -jnp.log(10000.0) * jnp.arange(half_width, dtype=jnp.int32).astype(f32) / half_width
    )
    angles = places.astype(f32)[:, None] * frequency[None, :]
    cosine, sine = jnp.cos(angles), jnp.sin(angles)
    cos_wide = jnp.tile(jnp.concatenate([cosine, cosine], axis=1), (1, heads))
    sin_wide = jnp.tile(jnp.concatenate([-sine, sine], axis=1), (1, heads))
    limit = jnp.maximum(places, prefixes[0] - 1)

    sizes = (heads, at_q, at_kv, at_gain, at_up, chunks_up, up_rows, query_scale)
    normed_all, q_nope, q_rope, compressed, latent, key_rope, key_value = front(
        x_all, weight_front, cos_wide, sin_wide, gain_latent, sizes
    )
    go_all = jnp.concatenate([after(block, q_nope) for block in go_blocks], axis=0)
    go_own, go_far = dispatch(go_all)
    attended = [None] * peers
    out_parts = [None] * peers
    for k in list(range(peers - 1, -1, -1)):
        attended[k], part = attend(
            q_nope,
            q_rope,
            key_rope,
            key_value,
            places[None, :],
            limit[:, None],
            weight_front,
            k,
            local_rows,
            bf16 if k else f32,
        )
        out_parts[k] = send_back(part, k)

    x_here = block_input.astype(f32)
    middle = after(x_here + out_parts[0], go_own)
    middle = middle + sum(part.astype(f32) for part in out_parts[1:])
    normed_two = norm_rows(middle, gain_two).astype(bf16)
    h2 = jnp.concatenate(gather_rows(normed_two), axis=0)

    def blocks_of(array):
        return [array[k * local_rows : (k + 1) * local_rows] for k in range(peers)]

    gathers = [None] + [Gather(p.reshape(2, 3 * e_cols, d_rows)) for p in pieces[1:]]
    gets, sums = Flow(), Flow()
    gets.add(*gathers[1:2])
    (h2,) = gets.tick(h2)
    (ffn_part,), (h2_grad,), grad_shared, _ = ffn(
        [h2], [go_all], jnp.ones((1, rows), f32), shared_full, None, f32
    )
    grad_shared, h2 = gets.tick(grad_shared, h2)
    pair, h2 = sync([], pair_sums(grad_shared), h2)
    shared_chain = Chain(pair)
    sums.start(shared_chain)

    router = jax.nn.softmax(dot_nt(h2, router_full), axis=-1)
    route_gates = jnp.sum(
        jnp.where(routes_mine[:, :, None] == expert_ids, router[:, None, :], 0.0), axis=2
    )

    def slot_gates(ids):
        return jnp.sum(
            jnp.where(flat_slot[:, 0:1] == ids[None, :], route_gates[:, 0:1], 0.0)
            + jnp.where(flat_slot[:, 1:2] == ids[None, :], route_gates[:, 1:2], 0.0),
            axis=0,
        )

    gate_own = slot_gates(own_ids).reshape(half, capacity)
    gate_far = swap_core(slot_gates(far_ids).reshape(half, capacity))
    xe_own, xe_far = dispatch(h2)
    xe_own, gate_own = gets.tick(xe_own, gate_own)

    gate_grads, outs_own, outs_far, chains = [], [], [], []

    def expert(s, weight, gate_own):
        gates = jnp.concatenate([gate_own[s : s + 1], gate_far[s : s + 1]], axis=1)
        outs, backs, grad, gate_grad = ffn(
            [xe_own, xe_far], [go_own, go_far], gates, weight, s, bf16
        )
        gate_grads.append(gate_grad)
        outs_own.append(outs[0])
        outs_far.append(outs[1])
        return backs[0], backs[1], grad

    def ids_of(s):
        base = jnp.arange(capacity, dtype=jnp.int32)[None, :] + s * capacity
        return [core * slots + base, (1 - core) * slots + base]

    here, there, grad = expert(0, expert_full[0], gate_own)
    for s in range(half - 1):
        here, there = sums.tick(here, there)
        gets.add(*gathers[s + 2 : s + 3])
        here, there = gets.tick(here, there)
        h2_grad = combine(
            h2_grad, flat_slot, ids_of(s), [here, swap_core(there)], local_rows, 0, peers, f32
        )
        weight = gathers[s + 1].result().reshape(expert_full[0].shape)
        weight, h2_grad, gate_own = sync([], weight, h2_grad, gate_own)
        chains.append(Chain(grad))
        sums.add(chains[-1])
        here, there, grad = expert(s + 1, weight, gate_own)
        if s + 2 < half:
            here, there = gets.tick(here, there)
            here, there = sums.tick(here, there)
            here, there = gets.tick(here, there)
    there = swap_core(there)
    h2_parts = [None] * peers
    for k in range(peers - 1, -1, -1):
        part = combine(
            h2_grad, flat_slot, ids_of(half - 1), [here, there], local_rows, k, 1, bf16 if k else f32
        )
        h2_parts[k] = send_back(part, k)
    gate_grads = jnp.concatenate(gate_grads, axis=0)
    gate_grad_mine = gate_grads[:, :capacity].reshape(-1)
    gate_grad_here = swap_core(gate_grads[:, capacity:]).reshape(-1)
    gate_tokens = jnp.stack(
        [
            jnp.sum(
                jnp.where(flat_slot[:, k : k + 1] == own_ids[None, :], gate_grad_mine[None, :], 0.0)
                + jnp.where(
                    flat_slot[:, k : k + 1] == far_ids[None, :], gate_grad_here[None, :], 0.0
                ),
                axis=1,
            )
            for k in range(TOP)
        ],
        axis=1,
    )
    gates_here = sum_rows(blocks_of(gate_tokens))

    chains.append(Chain(grad))
    sums.add(chains[-1])
    ffn_part, own_part = sums.tick(ffn_part, h2_parts[0])
    out_here = [swap_core(o) for o in outs_far]
    ffn_part = combine(
        ffn_part,
        flat_slot,
        [i for s in range(half) for i in ids_of(s)],
        [o for pair in zip(outs_own, out_here) for o in pair],
        local_rows,
        0,
        peers,
        bf16,
    )
    own_part, ffn_part = sums.tick(own_part, ffn_part)
    h2_grad_here = own_part + sum(part.astype(f32) for part in h2_parts[1:])

    router_here = router[:local_rows]
    route_grad = gates_here * kept_mine[:local_rows]
    router_grad = jnp.sum(
        jnp.where(
            routes_mine[:local_rows, :, None] == expert_ids, route_grad[:, :, None], 0.0
        ),
        axis=1,
    )
    logit_grad = (
        router_here * (router_grad - jnp.sum(router_here * router_grad, axis=-1, keepdims=True))
    ).astype(bf16)
    h2_grad_here = h2_grad_here + dot(logit_grad, router_full)
    middle_norm_grad, grad_gain_two = norm_back(middle, gain_two, h2_grad_here)
    middle_grad = out_grad.astype(f32) + middle_norm_grad
    attn_grad = gather_rows(middle_grad.astype(bf16))

    h1_parts = [None] * peers
    query_grads = [None] * peers
    so_far = None
    finished = []
    for k in range(peers):
        query_grads[k], part, dkv, dkr = attend_back(
            attn_grad[k],
            q_nope,
            q_rope,
            key_rope,
            key_value,
            places[:, None],
            limit[None, :],
            cos_wide,
            sin_wide,
            weight_front,
            so_far,
            k,
            query_scale,
            bf16 if k else f32,
        )
        h1_parts[k] = send_back(part, k)
        if k == 0:
            dkv, dkr = sums.tick(dkv, dkr)
            finished = [shared_chain.result()] + [c.result().astype(bf16) for c in chains[:-1]]
            dkv, *finished = sync([], dkv, *finished)
        so_far = (dkv, dkr)

    kv_grad, compressed_grad, grad_gain_latent = latent_back(
        dkv, dkr, compressed, cos_wide, sin_wide, gain_latent, weight_front, at_up, chunks_up, up_rows
    )
    compressed_parts = [send_back(part, k) for k, part in enumerate(blocks_of(compressed_grad))]
    wide = KVR + 2 * ROPE
    small_grad = outer([compressed_grad], [normed_all], d_rows)
    gain_rows = jnp.stack(
        [
            grad_gain_two.reshape(dp_count, d_rows),
            jnp.pad(
                grad_gain_latent.reshape(dp_count, peers, kv_gain.shape[0]),
                ((0, 0), (0, 0), (0, small_rows - kv_gain.shape[0])),
            ).reshape(dp_count, d_rows),
        ],
        axis=1,
    )
    router_rows = jnp.swapaxes(dot_tn(logit_grad, normed_two).reshape(experts, dp_count, d_rows), 0, 1)
    extra_rows = jnp.concatenate([router_rows, gain_rows], axis=1).astype(bf16)
    extra_rows = jnp.pad(extra_rows, ((0, 0), (0, wide - kv_cols - extra_rows.shape[1]), (0, 0)))
    small_grad = jnp.concatenate([small_grad[:, :kv_cols], extra_rows], axis=1)
    share = wide // peers
    small_parts = [
        send_back(lax.dynamic_slice_in_dim(small_grad, (me ^ k) * share, share, 1), k)
        for k in range(peers)
    ]

    query_grad = outer(query_grads, blocks_of(after(normed_all, small_parts[0])), d_rows)
    pair, kv_grad = sums.tick(pair_sums(query_grad), kv_grad)
    query_chain = Chain(pair)
    sums.start(query_chain)
    up_grad = outer([latent], [kv_grad], d_rows).reshape(chunks_up, dp_count, up_rows, d_rows)
    up_grad = jnp.swapaxes(up_grad, 0, 1).reshape(dp_count, chunks_up * up_rows, d_rows)
    out_grads = outer(attended, attn_grad, d_rows)
    small_mine = sum(part.astype(f32) for part in small_parts).astype(bf16)
    late_grad = jnp.concatenate([out_grads, up_grad, small_mine], axis=1)
    pair, own_part = sync([], pair_sums(late_grad), h1_parts[0])
    late_chain = Chain(pair)
    sums.start(late_chain)

    compressed_round = sum(part.astype(f32) for part in compressed_parts).astype(bf16)[:, :kv_cols]
    down_full = jnp.swapaxes(weight_front[:, at_kv:at_router, :], 0, 1).reshape(kv_cols, D)
    h1_grad = own_part + sum(part.astype(f32) for part in h1_parts[1:])
    h1_grad = h1_grad + dot(compressed_round, down_full)
    input_norm_grad, _ = norm_back(x_here, gain_one, h1_grad)
    input_grad = middle_grad + input_norm_grad
    input_grad, ffn_part = sums.tick(input_grad, ffn_part)
    output = (middle + sum_rows(blocks_of(ffn_part))).astype(bf16)

    shared_sum, *expert_sums = finished
    expert_sums.append(chains[-1].result().astype(bf16))
    query_sum, late_sum = query_chain.result(), late_chain.result()
    out_sum = late_sum[:at_q]
    query_chain_sum = query_sum
    nope_rows = heads * NOPE
    query_sum = jnp.concatenate(
        [
            query_sum[:nope_rows].reshape(heads, NOPE, d_rows),
            query_sum[nope_rows:].reshape(heads, ROPE, d_rows),
        ],
        axis=1,
    )
    query_sum = query_sum.reshape(q_cols, d_rows).T
    up_end = at_q + chunks_up * up_rows
    kvup_sum = jnp.swapaxes(
        late_sum[at_q:up_end].reshape(chunks_up, up_rows, d_rows), 0, 1
    ).reshape(up_rows, chunks_up * d_rows)

    small_sum = late_sum[up_end:]
    small_weight = jnp.pad(
        front_local[at_kv : at_kv + kv_cols].astype(f32), ((0, wide - kv_cols), (0, 0))
    )
    gain_part = jnp.sum(
        front_local[at_q:at_kv].astype(f32) * query_chain_sum, axis=0, keepdims=True
    ) + jnp.sum(
        lax.dynamic_slice_in_dim(small_weight, me * share, share, 0) * small_sum,
        axis=0,
        keepdims=True,
    )
    last = jnp.concatenate([small_sum, gain_part, jnp.zeros((7, d_rows), f32)], axis=0)
    by_peer = jnp.swapaxes(last.reshape(-1, peers, small_rows), 0, 1)
    last_parts = [
        send_back(lax.dynamic_index_in_dim(by_peer, me ^ k, 0, False), k) for k in range(peers)
    ]
    small_whole = jnp.zeros((wide, small_rows), f32)
    for k, part in enumerate(last_parts):
        small_whole = lax.dynamic_update_slice_in_dim(small_whole, part[:share], (me ^ k) * share, 0)
    gain_one_here = lax.dynamic_slice_in_dim(gain_one[0], (place * peers + me) * small_rows, small_rows)
    gain_one_out = sum(part[share] for part in last_parts) / gain_one_here
    kv_out = small_whole[:kv_cols].T
    router_out = small_whole[kv_cols : kv_cols + experts].T
    gain_two_out = small_whole[kv_cols + experts]
    gain_latent_out = small_whole[kv_cols + experts + 1, : kv_gain.shape[0]]

    mine = [lax.dynamic_index_in_dim(e, core, 0, False) for e in expert_sums]
    theirs = [swap_core(lax.dynamic_index_in_dim(e, 1 - core, 0, False)) for e in expert_sums]
    expert_grad = jnp.stack(
        [jnp.where(first, a, b) for a, b in zip(mine, theirs)]
        + [jnp.where(first, b, a) for a, b in zip(mine, theirs)],
        axis=0,
    ).astype(f32)

    return (
        output,
        input_grad,
        gain_one_out,
        query_sum,
        kv_out,
        gain_latent_out,
        kvup_sum,
        out_sum,
        gain_two_out,
        router_out,
        shared_sum[:s_cols].T,
        shared_sum[s_cols : 2 * s_cols].T,
        shared_sum[2 * s_cols :],
        jnp.swapaxes(expert_grad[:, :e_cols], 1, 2),
        jnp.swapaxes(expert_grad[:, e_cols : 2 * e_cols], 1, 2),
        expert_grad[:, 2 * e_cols :],
    )


def solution(mesh):
    placed = (
        P(("dp", "tensor"), None),
        P(("dp", "tensor"), None),
        P("dp", None),
        P("dp"),
        P("dp", None),
        P(("dp", "tensor")),
        P("dp", "tensor"),
        P(("dp", "tensor"), None),
        P(("dp", "tensor")),
        P("dp", "tensor"),
        P("tensor", "dp"),
        P(("dp", "tensor")),
        P(("dp", "tensor"), None),
        P("dp", "tensor"),
        P("dp", "tensor"),
        P("tensor", "dp"),
        P(None, "dp", "tensor"),
        P(None, "dp", "tensor"),
        P(None, "tensor", "dp"),
    )
    return jax.shard_map(
        on_device,
        mesh=mesh,
        in_specs=placed,
        out_specs=(
            P(("dp", "tensor"), None),
            P(("dp", "tensor"), None),
            P(("dp", "tensor")),
            P("dp", "tensor"),
            P(("dp", "tensor"), None),
            P(("dp", "tensor")),
            P("dp", "tensor"),
            P("tensor", "dp"),
            P(("dp", "tensor")),
            P(("dp", "tensor"), None),
            P("dp", "tensor"),
            P("dp", "tensor"),
            P("tensor", "dp"),
            P(None, "dp", "tensor"),
            P(None, "dp", "tensor"),
            P(None, "tensor", "dp"),
        ),
        check_vma=False,
    )
```

```python
import functools

import jax
import jax.numpy as jnp
from jax import lax
from jax.experimental import pallas as pl
from jax.experimental.pallas import tpu as pltpu
from jax.sharding import PartitionSpec as P

D = 2048
NOPE = 128
ROPE = 64
VD = 128
KVR = 512
TOP = 2
LENGTH = 1024

eps = 1e-06
bf16 = jnp.bfloat16
f32 = jnp.float32


def dot(a, b, dims=((1,), (0,)), out=f32):
    return lax.dot_general(a, b, (dims, ((), ())), preferred_element_type=f32).astype(out)


def dot_nt(a, b, out=f32):
    return dot(a, b, ((1,), (1,)), out)


def dot_tn(a, b, out=f32):
    return dot(a, b, ((0,), (0,)), out)


def inv_rms(values):
    return lax.rsqrt(jnp.mean(values * values, axis=-1, keepdims=True) + eps)


def norm_rows(values, gain_vec):
    return values * inv_rms(values) * gain_vec


def norm_back(values, gain_vec, upstream):
    inv = inv_rms(values)
    scaled = upstream * gain_vec
    grad = inv * scaled - values * (
        inv * inv * inv * jnp.mean(values * scaled, axis=-1, keepdims=True)
    )
    return grad, jnp.sum(upstream * values * inv, axis=0)


def swap_core(values):
    count = lax.axis_size("dp")
    return lax.ppermute(values, "dp", [(i, i ^ 1) for i in range(count)])


def gather_rows(values):
    count = lax.axis_size("tensor")
    return [values] + [
        lax.ppermute(values, "tensor", [(i, i ^ k) for i in range(count)])
        for k in range(count - 1, 0, -1)
    ][::-1]


def far_halves(near):
    cut = near[0].shape[0] // 2
    return [send_back(near[0][:cut], 2), send_back(near[1][cut:], 1)]


def send_back(part, k):
    count = lax.axis_size("tensor")
    return part if k == 0 else lax.ppermute(part, "tensor", [(i, i ^ k) for i in range(count)])


def sum_rows(blocks):
    count = lax.axis_size("tensor")
    total = blocks[0].astype(f32)
    arrived = [
        lax.ppermute(blocks[k].astype(bf16), "tensor", [(i, i ^ k) for i in range(count)])
        for k in range(count - 1, 0, -1)
    ]
    for piece in arrived:
        total = total + piece.astype(f32)
    return total


NT=(((1,),(1,)),((),())); NN=(((1,),(0,)),((),()))
def mm(a,b,dims=NN): return lax.dot_general(a,b,dims,preferred_element_type=f32)

def ffn_kernel(parts, hidden_cols, *refs):
    x_refs=refs[:parts]; g_refs=refs[parts:2*parts]; gate_ref, w_ref = refs[2*parts:2*parts+2]
    outs=refs[2*parts+2:]
    out_refs=outs[:parts]; back_refs=outs[parts:2*parts]; grad_ref, dgate_ref = outs[2*parts:2*parts+2]
    val, raw, back_t, gated_t, back_n, gated_n = outs[2*parts+2:]
    phase=pl.program_id(0); step=pl.program_id(1)
    F=hidden_cols
    def rows_of(rs):
        pieces=[r[...].reshape(r.shape[-2:]) for r in rs]
        return pieces[0] if parts==1 else jnp.concatenate(pieces,axis=0)
    x=rows_of(x_refs); g=rows_of(g_refs)
    w=w_ref[...].reshape(w_ref.shape[-2:])
    @pl.when(phase==0)
    def _():
        a=mm(w[:2*F],x,NT); b=mm(w[2*F:],g,NT)
        @pl.when(step==0)
        def _():
            val[...]=a; raw[...]=b
        @pl.when(step>0)
        def _():
            val[...]+=a; raw[...]+=b
    @pl.when((phase==1)&(step==0))
    def _():
        eg=val[:F]; eu=val[F:]; r=raw[...]; gate=gate_ref[...]
        s=jax.nn.sigmoid(eg); act=eg*s
        hid=(act*eu).astype(bf16).astype(f32)
        dgate_ref[...]=jnp.sum(hid*r,axis=0,keepdims=True)
        gated=(hid*gate).astype(bf16)
        d=r*gate
        bg=(d*eu*s*(1.0+eg*(1.0-s))).astype(bf16); bu=(d*act).astype(bf16)
        back_t[:F]=bg; back_t[F:]=bu; gated_t[...]=gated
        back_n[...]=back_t[...].T; gated_n[...]=gated.T
    @pl.when(phase==1)
    def _():
        o=mm(gated_n[...],w[2*F:]); b=mm(back_n[...],w[:2*F])
        at=0
        for ro,rb in zip(out_refs,back_refs):
            n=ro.shape[-2]
            ro[...]=o[at:at+n].astype(ro.dtype).reshape(ro.shape); rb[...]=b[at:at+n].astype(rb.dtype).reshape(rb.shape); at+=n
        sh=grad_ref.shape[:-2]
        gr=jnp.concatenate([mm(back_t[...],x),mm(gated_t[...],g)],axis=0).astype(bf16)
        grad_ref[...]=gr.reshape(grad_ref.shape)

def ffn(xs, gs, gates, w, stage, out_dtype):
    parts=len(xs)
    F=w.shape[-2]//3; dl=w.shape[-1]
    D=xs[0].shape[-1]; nd=D//dl
    ns=[x.shape[-2] for x in xs]; n=sum(ns)
    if stage is None:
        row_spec=[pl.BlockSpec((m,dl),lambda p,j:(0,j)) for m in ns]
        w_spec=pl.BlockSpec((1,3*F,dl),lambda p,j:(j,0,0))
        g_shape=(nd,3*F,dl); g_spec=pl.BlockSpec((1,3*F,dl),lambda p,j:(j*p,0,0))
    else:
        row_spec=[pl.BlockSpec((1,m,dl),lambda p,j:(stage,0,j)) for m in ns]
        ws=stage%w.shape[1]
        w_spec=pl.BlockSpec((1,1,1,3*F,dl),lambda p,j:(j//2,ws,j%2,0,0))
        g_shape=(nd//2,2,3*F,dl); g_spec=pl.BlockSpec((1,1,3*F,dl),lambda p,j:((j*p)//2,(j*p)%2,0,0))
    out_spec=[pl.BlockSpec((m,dl),lambda p,j:(0,j*p)) for m in ns]
    flops=2*n*D*F*9
    res = pl.pallas_call(
        functools.partial(ffn_kernel,parts,F),
        grid=(2,nd),
        in_specs=row_spec*2+[pl.BlockSpec((1,n),lambda p,j:(0,0)),w_spec],
        out_specs=out_spec*2+[g_spec,pl.BlockSpec((1,n),lambda p,j:(0,0))],
        out_shape=[jax.ShapeDtypeStruct((m,D),out_dtype) for m in ns]*2+[jax.ShapeDtypeStruct(g_shape,bf16),jax.ShapeDtypeStruct((1,n),f32)],
        scratch_shapes=[pltpu.VMEM((2*F,n),f32),pltpu.VMEM((F,n),f32),pltpu.VMEM((2*F,n),bf16),pltpu.VMEM((F,n),bf16),pltpu.VMEM((n,2*F),bf16),pltpu.VMEM((n,F),bf16)],
        compiler_params=pltpu.CompilerParams(dimension_semantics=("arbitrary","arbitrary"),vmem_limit_bytes=60*1024*1024),
        cost_estimate=pl.CostEstimate(flops=flops,bytes_accessed=2*3*F*D*3+2*n*D*6,transcendentals=n*F),
        name="ffn",
    )(*xs,*gs,gates,w)
    return res[:parts], res[parts:2*parts], res[2*parts], res[2*parts+1]


def front_kernel(sizes, x_ref, w_ref, cos_ref, sin_ref, gl_ref, h_ref, qn_ref, qr_ref, comp_ref, lat_ref, kr_ref, kv_ref, extra, ups):
    heads, at_q, at_kv, at_gain, at_up, chunks, up_rows, scale = sizes
    nd, _, dl = w_ref.shape
    qn_cols, qr_cols = heads * NOPE, heads * ROPE
    half = ROPE // 2
    main = qn_cols + qr_cols + KVR

    @pl.when(pl.program_id(0) == 0)
    def _():
        for j in range(nd):
            w_r = w_ref[j, at_q + qn_cols : at_q + qn_cols + qr_cols, :]
            w_k = w_ref[j, at_kv + KVR : at_kv + KVR + ROPE, :]
            swapped = []
            for h in range(heads):
                swapped.append(w_r[h * ROPE + half : (h + 1) * ROPE])
                swapped.append(w_r[h * ROPE : h * ROPE + half])
            extra[j] = jnp.concatenate(
                swapped + [w_k, w_k, w_k[half:], w_k[:half], w_k[half:], w_k[:half]], axis=0
            )
            for c in range(chunks):
                at = at_up + c * up_rows
                ups[c, j * up_rows : (j + 1) * up_rows, :] = w_ref[j, at : at + up_rows, :]

    x = x_ref[...].astype(f32)
    inv = lax.rsqrt(jnp.mean(x * x, axis=-1, keepdims=True) + eps)
    acc = None
    for j in range(nd):
        gain = w_ref[j, at_gain : at_gain + 16, :][0:1].astype(f32)
        h = (x[:, j * dl : (j + 1) * dl] * inv * gain).astype(bf16)
        h_ref[:, j * dl : (j + 1) * dl] = h
        part = [mm(h, w_ref[j, at_q : at_q + main, :], NT), mm(h, extra[j], NT)]
        acc = part if acc is None else [a + b for a, b in zip(acc, part)]
    a, b = acc
    cos, sin = cos_ref[...], sin_ref[...]
    qn_ref[...] = (a[:, :qn_cols] * scale).astype(bf16)
    qr_ref[...] = (
        (a[:, qn_cols : qn_cols + qr_cols] * cos + b[:, :qr_cols] * sin) * scale
    ).astype(bf16)
    comp = a[:, qn_cols + qr_cols :]
    comp_ref[...] = comp
    wide = 2 * ROPE
    kr_ref[...] = (
        b[:, qr_cols : qr_cols + wide] * cos[:, :wide]
        + b[:, qr_cols + wide : qr_cols + 2 * wide] * sin[:, :wide]
    ).astype(bf16)
    lat = (
        comp * lax.rsqrt(jnp.mean(comp * comp, axis=-1, keepdims=True) + eps) * gl_ref[...]
    ).astype(bf16)
    lat_ref[...] = lat
    for c in range(chunks):
        kv_ref[:, c * dl : (c + 1) * dl] = mm(lat, ups[c]).astype(bf16)


def front(x, w, cos, sin, gain_latent, sizes):
    heads, at_q, at_kv, at_gain, at_up, chunks, up_rows, scale = sizes
    rows, width = x.shape
    nd, _, dl = w.shape
    tb = min(256, rows)
    row = lambda cols: pl.BlockSpec((tb, cols), lambda i: (i, 0))
    whole = lambda a: pl.BlockSpec(a.shape, lambda i: (0,) * a.ndim)
    cols = [width, heads * NOPE, heads * ROPE, KVR, KVR, 2 * ROPE, heads * (NOPE + VD)]
    kinds = [bf16, bf16, bf16, f32, bf16, bf16, bf16]
    return pl.pallas_call(
        functools.partial(front_kernel, sizes),
        grid=(rows // tb,),
        in_specs=[row(width), whole(w), row(heads * ROPE), row(heads * ROPE), whole(gain_latent)],
        out_specs=[row(c) for c in cols],
        out_shape=[jax.ShapeDtypeStruct((rows, c), k) for c, k in zip(cols, kinds)],
        scratch_shapes=[
            pltpu.VMEM((nd, heads * ROPE + 4 * ROPE, dl), bf16),
            pltpu.VMEM((chunks, nd * up_rows, dl), bf16),
        ],
        compiler_params=pltpu.CompilerParams(vmem_limit_bytes=60 * 1024 * 1024),
        cost_estimate=pl.CostEstimate(
            flops=2 * rows * width * 1900, bytes_accessed=2 * w.size + 12 * rows * width, transcendentals=0
        ),
        name="front",
    )(x, w, cos, sin, gain_latent)


def head_rope(wide, h):
    lane = lax.broadcasted_iota(jnp.int32, wide.shape, 1)
    return jnp.where((lane // ROPE) == (h % 2), wide, jnp.zeros_like(wide))


def attend_kernel(heads, qn_ref, qr_ref, kr_ref, kv_ref, kpos_ref, lim_ref, w_ref, att_ref, out_ref):
    kr = kr_ref[...]
    keep = kpos_ref[...] <= lim_ref[...]
    wide = 2 * ROPE
    for h in range(heads):
        at = h * (NOPE + VD)
        q = jnp.concatenate(
            [
                qn_ref[:, h * NOPE : (h + 1) * NOPE],
                head_rope(qr_ref[:, (h // 2) * wide : (h // 2 + 1) * wide], h),
            ],
            axis=1,
        )
        k = jnp.concatenate([kv_ref[:, at : at + NOPE], kr], axis=1)
        s = jnp.where(keep, mm(q, k, NT), -1e30)
        p = jnp.exp(s - jnp.max(s, axis=1, keepdims=True))
        p = (p * (1.0 / jnp.sum(p, axis=1, keepdims=True))).astype(bf16)
        att_ref[:, h * VD : (h + 1) * VD] = mm(p, kv_ref[:, at + NOPE : at + NOPE + VD]).astype(bf16)
    att = att_ref[...]
    dl = w_ref.shape[2]
    for j in range(w_ref.shape[0]):
        out_ref[:, j * dl : (j + 1) * dl] = mm(att, w_ref[j]).astype(out_ref.dtype)


def attend(qn, qr, kr, kv, kpos, limit, w, block, block_rows, out_dtype):
    rows = qn.shape[0]
    heads = qn.shape[1] // NOPE
    nd, _, dl = w.shape
    row = lambda cols: pl.BlockSpec((block_rows, cols), lambda i: (block, 0))
    whole = lambda a: pl.BlockSpec(a.shape, lambda i: (0,) * a.ndim)
    first = lambda cols: pl.BlockSpec((block_rows, cols), lambda i: (0, 0))
    return pl.pallas_call(
        functools.partial(attend_kernel, heads),
        grid=(1,),
        in_specs=[
            row(heads * NOPE),
            row(heads * ROPE),
            whole(kr),
            whole(kv),
            whole(kpos),
            row(1),
            pl.BlockSpec((nd, heads * VD, dl), lambda i: (0, 0, 0)),
        ],
        out_specs=[first(heads * VD), first(nd * dl)],
        out_shape=[
            jax.ShapeDtypeStruct((block_rows, heads * VD), bf16),
            jax.ShapeDtypeStruct((block_rows, nd * dl), out_dtype),
        ],
        compiler_params=pltpu.CompilerParams(vmem_limit_bytes=60 * 1024 * 1024),
        cost_estimate=pl.CostEstimate(
            flops=2 * block_rows * heads * (rows * 384 + VD * nd * dl),
            bytes_accessed=8 * 1024 * 1024,
            transcendentals=block_rows * heads * rows,
        ),
        name="attend",
    )(qn, qr, kr, kv, kpos, limit, w)


def rot_back(v, cos, sin):
    half = ROPE // 2
    lane = lax.broadcasted_iota(jnp.int32, v.shape, 1)
    width = v.shape[1]
    down = pltpu.roll(v, width - half, 1)
    up = pltpu.roll(v, half, 1)
    other = jnp.where(lane % ROPE < half, down, up)
    return v * cos - other * sin


def attend_back_kernel(heads, scale, first, *refs):
    da_ref, qn_ref, qr_ref, kr_ref, kv_ref, kpos_ref, lim_ref, cos_ref, sin_ref = refs[:9]
    wo_ref, wa_ref, wb_ref, wr_ref = refs[9:13]
    dkv_in, dkr_in = (None, None) if first else refs[13:15]
    dq_ref, dh_ref, dkv_ref, dkr_ref = refs[13 if first else 15 :]
    nd, _, dl = wo_ref.shape
    wide = 2 * ROPE
    width = NOPE + VD
    grad = None
    for j in range(nd):
        part = mm(da_ref[:, j * dl : (j + 1) * dl], wo_ref[j], NT)
        grad = part if grad is None else grad + part
    grad = grad.astype(bf16)
    kr = kr_ref[...]
    keep = kpos_ref[...] <= lim_ref[...]
    rope_grads = []
    dkr = jnp.zeros(dkr_ref.shape, f32) if first else dkr_in[...]
    for h in range(heads):
        at = h * width
        q = jnp.concatenate(
            [
                qn_ref[:, h * NOPE : (h + 1) * NOPE],
                head_rope(qr_ref[:, (h // 2) * wide : (h // 2 + 1) * wide], h),
            ],
            axis=1,
        )
        k = jnp.concatenate([kv_ref[:, at : at + NOPE], kr], axis=1)
        do = grad[:, h * VD : (h + 1) * VD]
        s = jnp.where(keep, mm(k, q, NT), -1e30)
        p = jnp.exp(s - jnp.max(s, axis=0, keepdims=True))
        p = p * (1.0 / jnp.sum(p, axis=0, keepdims=True))
        dp = mm(kv_ref[:, at + NOPE : at + width], do, NT)
        ds = (p * (dp - jnp.sum(p * dp, axis=0, keepdims=True))).astype(bf16)
        dv = mm(p.astype(bf16), do)
        dk = mm(ds, q)
        if first:
            dkv_ref[:, at : at + NOPE] = dk[:, :NOPE]
            dkv_ref[:, at + NOPE : at + width] = dv
        else:
            dkv_ref[:, at : at + NOPE] = dkv_in[:, at : at + NOPE] + dk[:, :NOPE]
            dkv_ref[:, at + NOPE : at + width] = dkv_in[:, at + NOPE : at + width] + dv
        dkr = dkr + dk[:, NOPE:]
        dq = lax.dot_general(ds, k, (((0,), (0,)), ((), ())), preferred_element_type=f32)
        dq_ref[:, h * NOPE : (h + 1) * NOPE] = (dq[:, :NOPE] * scale).astype(bf16)
        masked = head_rope(dq[:, NOPE:], h)
        if h % 2:
            rope_grads[-1] = rope_grads[-1] + masked
        else:
            rope_grads.append(masked)
    dkr_ref[...] = dkr
    ropes = rope_grads[0] if len(rope_grads) == 1 else jnp.concatenate(rope_grads, axis=1)
    at = heads * NOPE
    dq_ref[:, at:] = (rot_back(ropes, cos_ref[...], sin_ref[...]) * scale).astype(bf16)
    half = at // 2
    for j in range(nd):
        dh_ref[:, j * dl : (j + 1) * dl] = (
            mm(dq_ref[:, :half], wa_ref[j])
            + mm(dq_ref[:, half:at], wb_ref[j])
            + mm(dq_ref[:, at:], wr_ref[j])
        ).astype(dh_ref.dtype)


def attend_back(da, qn, qr, kr, kv, kpos, limit, cos, sin, w, so_far, block, scale, out_dtype):
    block_rows = da.shape[0]
    rows = qn.shape[0]
    heads = qn.shape[1] // NOPE
    nd, _, dl = w.shape
    row = lambda cols: pl.BlockSpec((block_rows, cols), lambda i: (block, 0))
    whole = lambda a: pl.BlockSpec(a.shape, lambda i: (0,) * a.ndim)
    rows_w = lambda size, at: pl.BlockSpec((nd, size, dl), lambda i: (0, at, 0))
    part = heads * ROPE
    dkv = jax.ShapeDtypeStruct((rows, heads * (NOPE + VD)), f32)
    dkr = jax.ShapeDtypeStruct((rows, 2 * ROPE), f32)
    first = so_far is None
    return pl.pallas_call(
        functools.partial(attend_back_kernel, heads, scale, first),
        grid=(1,),
        in_specs=[
            whole(da),
            row(heads * NOPE),
            row(heads * ROPE),
            whole(kr),
            whole(kv),
            whole(kpos),
            pl.BlockSpec((1, block_rows), lambda i: (0, block)),
            row(heads * ROPE),
            row(heads * ROPE),
            rows_w(2 * part, 0),
            rows_w(part, 2),
            rows_w(part, 3),
            rows_w(part, 4),
        ]
        + ([] if first else [whole(dkv), whole(dkr)]),
        out_specs=[
            pl.BlockSpec((block_rows, 3 * part), lambda i: (0, 0)),
            pl.BlockSpec((block_rows, nd * dl), lambda i: (0, 0)),
            whole(dkv),
            whole(dkr),
        ],
        out_shape=[
            jax.ShapeDtypeStruct((block_rows, 3 * part), bf16),
            jax.ShapeDtypeStruct((block_rows, nd * dl), out_dtype),
            dkv,
            dkr,
        ],
        input_output_aliases={} if first else {13: 2, 14: 3},
        compiler_params=pltpu.CompilerParams(vmem_limit_bytes=60 * 1024 * 1024),
        cost_estimate=pl.CostEstimate(
            flops=2 * block_rows * heads * (rows * 1024 + 5 * ROPE * nd * dl),
            bytes_accessed=20 * 1024 * 1024,
            transcendentals=block_rows * heads * rows,
        ),
        name="attend_back",
    )(da, qn, qr, kr, kv, kpos, limit, cos, sin, w, w, w, w, *(() if first else so_far))


def latent_back_kernel(sizes, dkv_ref, dkr_ref, comp_ref, cos_ref, sin_ref, gl_ref, w_ref, dkvb_ref, dc_ref, dg_ref, ups):
    chunks, up_rows, in_rows = sizes
    nd, _, dl = w_ref.shape
    dkv = dkv_ref[...].astype(bf16)
    dkvb_ref[...] = dkv

    @pl.when(pl.program_id(0) == 0)
    def _():
        for j in range(nd):
            for c in range(chunks):
                at = in_rows + c * up_rows
                ups[c, j * up_rows : (j + 1) * up_rows, :] = w_ref[j, at : at + up_rows, :]

    dlat = None
    for c in range(chunks):
        part = mm(dkv[:, c * dl : (c + 1) * dl], ups[c], NT)
        dlat = part if dlat is None else dlat + part
    comp = comp_ref[...]
    inv = lax.rsqrt(jnp.mean(comp * comp, axis=-1, keepdims=True) + eps)
    scaled = dlat * gl_ref[...]
    dc_ref[:, :KVR] = (
        inv * scaled - comp * (inv * inv * inv * jnp.mean(comp * scaled, axis=-1, keepdims=True))
    ).astype(dc_ref.dtype)
    dg = jnp.sum(dlat * comp * inv, axis=0, keepdims=True)

    @pl.when(pl.program_id(0) == 0)
    def _():
        dg_ref[...] = dg

    @pl.when(pl.program_id(0) > 0)
    def _():
        dg_ref[...] += dg

    dkr = dkr_ref[...]
    dkr = dkr + pltpu.roll(dkr, ROPE, 1)
    wide = 2 * ROPE
    dkr = rot_back(dkr, cos_ref[:, :wide], sin_ref[:, :wide])
    lane = lax.broadcasted_iota(jnp.int32, dkr.shape, 1)
    dc_ref[:, KVR:] = jnp.where(lane < ROPE, dkr, 0.0).astype(dc_ref.dtype)


def latent_back(dkv, dkr, comp, cos, sin, gain_latent, w, at_up, chunks, up_rows):
    rows = dkv.shape[0]
    nd, _, dl = w.shape
    tb = min(256, rows)
    row = lambda cols: pl.BlockSpec((tb, cols), lambda i: (i, 0))
    whole = lambda a: pl.BlockSpec(a.shape, lambda i: (0,) * a.ndim)
    return pl.pallas_call(
        functools.partial(latent_back_kernel, (chunks, up_rows, at_up)),
        grid=(rows // tb,),
        in_specs=[
            row(dkv.shape[1]),
            row(dkr.shape[1]),
            row(KVR),
            row(cos.shape[1]),
            row(cos.shape[1]),
            whole(gain_latent),
            whole(w),
        ],
        out_specs=[row(dkv.shape[1]), row(KVR + 2 * ROPE), pl.BlockSpec((1, KVR), lambda i: (0, 0))],
        out_shape=[
            jax.ShapeDtypeStruct(dkv.shape, bf16),
            jax.ShapeDtypeStruct((rows, KVR + 2 * ROPE), bf16),
            jax.ShapeDtypeStruct((1, KVR), f32),
        ],
        scratch_shapes=[pltpu.VMEM((chunks, nd * up_rows, dl), bf16)],
        compiler_params=pltpu.CompilerParams(vmem_limit_bytes=60 * 1024 * 1024),
        cost_estimate=pl.CostEstimate(
            flops=2 * rows * KVR * dkv.shape[1], bytes_accessed=16 * 1024 * 1024, transcendentals=0
        ),
        name="latent_back",
    )(dkv, dkr, comp, cos, sin, gain_latent, w)


def outer_kernel(parts, *refs):
    a_refs, b_refs, out_ref, at_ref = refs[:parts], refs[parts : 2 * parts], refs[-2], refs[-1]

    @pl.when(pl.program_id(0) == 0)
    def _():
        at = 0
        for a in a_refs:
            at_ref[:, at : at + a.shape[0]] = a[...].T
            at += a.shape[0]

    right = b_refs[0][...] if parts == 1 else jnp.concatenate([b[...] for b in b_refs], axis=0)
    out_ref[...] = mm(at_ref[...], right).astype(bf16)[None]


def outer(left, right, width):
    parts = len(left)
    rows = sum(a.shape[0] for a in left)
    cols = left[0].shape[1]
    count = right[0].shape[1] // width
    return pl.pallas_call(
        functools.partial(outer_kernel, parts),
        grid=(count,),
        in_specs=[pl.BlockSpec(a.shape, lambda j: (0, 0)) for a in left]
        + [pl.BlockSpec((b.shape[0], width), lambda j: (0, j)) for b in right],
        out_specs=pl.BlockSpec((1, cols, width), lambda j: (j, 0, 0)),
        out_shape=jax.ShapeDtypeStruct((count, cols, width), bf16),
        scratch_shapes=[pltpu.VMEM((cols, rows), bf16)],
        compiler_params=pltpu.CompilerParams(vmem_limit_bytes=60 * 1024 * 1024),
        cost_estimate=pl.CostEstimate(
            flops=2 * rows * cols * count * width,
            bytes_accessed=2 * (rows * cols + (rows + cols) * count * width),
            transcendentals=0,
        ),
        name="outer",
    )(*left, *right)


def combine_kernel(parts, split, *refs):
    slot_ref, acc_ref = refs[:2]
    id_refs, row_refs, out_refs = refs[2 : 2 + parts], refs[2 + parts : 2 + 2 * parts], refs[2 + 2 * parts :]
    one, two = slot_ref[:, 0:1], slot_ref[:, 1:2]
    total = acc_ref[...].astype(f32)
    for ids, rows in zip(id_refs, row_refs):
        hot = ((one == ids[...]) | (two == ids[...])).astype(f32).astype(bf16)
        total = total + mm(hot, rows[...])
    if not split:
        out_refs[0][...] = total.astype(out_refs[0].dtype)
    else:
        for k, out in enumerate(out_refs):

            @pl.when(pl.program_id(0) == k)
            def _(out=out):
                out[...] = total.astype(out.dtype)


def combine(acc, slots, ids, rows, block_rows, out_dtypes):
    parts = len(ids)
    count, width = acc.shape[0] // block_rows, acc.shape[1]
    split = len(out_dtypes) > 1
    whole = lambda a: pl.BlockSpec(a.shape, lambda i: (0, 0))
    return pl.pallas_call(
        functools.partial(combine_kernel, parts, split),
        grid=(count,),
        in_specs=[
            pl.BlockSpec((block_rows, TOP), lambda i: (i, 0)),
            pl.BlockSpec((block_rows, width), lambda i: (i, 0)),
        ]
        + [whole(a) for a in ids]
        + [whole(a) for a in rows],
        out_specs=[
            pl.BlockSpec((block_rows, width), (lambda i: (0, 0)) if split else (lambda i: (i, 0)))
            for _ in out_dtypes
        ],
        out_shape=[
            jax.ShapeDtypeStruct((block_rows if split else count * block_rows, width), kind)
            for kind in out_dtypes
        ],
        compiler_params=pltpu.CompilerParams(vmem_limit_bytes=60 * 1024 * 1024),
        cost_estimate=pl.CostEstimate(flops=1000000, bytes_accessed=1000000, transcendentals=0),
        name="combine",
    )(slots, acc, *ids, *rows)


def after(values, *others):
    return lax.optimization_barrier((values, *others))[0]


def sync(chains, *values):
    live = [c.live for c in chains]
    live, values = lax.optimization_barrier((live, values))
    for c, v in zip(chains, live):
        c.live = v
    return values


def rising_pairs(low, high):
    return [(2 * j + c, 2 * j + 2 + c) for j in range(low, high) for c in range(2)]


def falling_pairs(low, high):
    return [(2 * j + c, 2 * j - 2 + c) for j in range(low, high) for c in range(2)]


class Chain:
    def __init__(self, blocks):
        self.blocks = blocks
        self.nz = lax.axis_size("dp") // 2
        self.place = lax.axis_index("dp") // 2
        self.live = (blocks,)
        self.done = 0

    def term(self, index):
        return lax.dynamic_index_in_dim(self.blocks, jnp.clip(index, 0, self.nz - 1), 0, False)

    def advance(self):
        nz, place, step = self.nz, self.place, self.done
        if step >= nz - 1:
            return
        if step == 0:
            self.blocks = self.live[0]
        up, down = self.term(nz - 1 - step + place), self.term(step - nz + 1 + place)
        if step > 0:
            up = (up.astype(f32) + self.live[0].astype(f32)).astype(bf16)
            down = (down.astype(f32) + self.live[1].astype(f32)).astype(bf16)
        self.live = (
            lax.ppermute(up, "dp", rising_pairs(0, min(step + 1, nz - 1))),
            lax.ppermute(down, "dp", falling_pairs(max(nz - 1 - step, 1), nz)),
        )
        self.done += 1

    def rest(self):
        while self.done < self.nz - 1:
            self.advance()

    def result(self):
        self.rest()
        if self.nz == 1:
            return self.blocks[0].astype(f32)
        return self.term(self.place).astype(f32) + self.live[0].astype(f32) + self.live[1].astype(f32)


class Gather:
    def __init__(self, block):
        self.block = block
        self.nz = lax.axis_size("dp") // 2
        self.place = lax.axis_index("dp") // 2
        self.live = (block, block)
        self.arrived = []
        self.done = 0

    def advance(self):
        nz, step = self.nz, self.done
        if step >= nz - 1:
            return
        if step > 0:
            self.arrived.append(self.live)
        self.live = (
            lax.ppermute(self.live[0], "dp", rising_pairs(step, nz - 1)),
            lax.ppermute(self.live[1], "dp", falling_pairs(1, nz - step)),
        )
        self.done += 1

    def rest(self):
        while self.done < self.nz - 1:
            self.advance()

    def result(self):
        self.rest()
        arrived = self.arrived + ([self.live] if self.nz > 1 else [])
        full = jnp.zeros((self.nz, *self.block.shape), self.block.dtype)
        put = lambda full, block, at: lax.dynamic_update_index_in_dim(
            full, block, jnp.clip(at, 0, self.nz - 1), 0
        )
        for step in range(len(arrived) - 1, -1, -1):
            full = put(full, arrived[step][0], self.place - 1 - step)
        for step in range(len(arrived) - 1, -1, -1):
            full = put(full, arrived[step][1], self.place + 1 + step)
        return put(full, self.block, self.place)


class Flow:
    def __init__(self):
        self.active = []

    def add(self, *items):
        self.active += items

    def start(self, item):
        item.advance()
        self.add(item)

    def tick(self, *values):
        values = sync(self.active, *values)
        self.active = [c for c in self.active if c.done < c.nz - 1]
        for c in self.active:
            c.advance()
        return values


def pair_sums(grad):
    count = lax.axis_size("dp")
    core = lax.axis_index("dp") % 2
    parts = grad.reshape(count // 2, 2, grad.shape[1], grad.shape[2])
    other = lax.dynamic_index_in_dim(parts, 1 - core, 1, False)
    mine = lax.dynamic_index_in_dim(parts, core, 1, False)
    return (mine.astype(f32) + swap_core(other).astype(f32)).astype(bf16)


def sum_dp(grad):
    flat = grad.reshape(-1, grad.shape[-1])
    return lax.psum_scatter(flat, "dp", scatter_dimension=0, tiled=True)


def sum_z(grad):
    count = lax.axis_size("dp")
    groups = [[2 * j + c for j in range(count // 2)] for c in range(2)]
    flat = grad.reshape(-1, grad.shape[-1])
    total = lax.psum_scatter(flat, "dp", scatter_dimension=0, tiled=True, axis_index_groups=groups)
    return total.reshape(2, *grad.shape[2:])


def on_device(
    block_input,
    out_grad,
    routes,
    prefixes,
    drop_order,
    attn_gain,
    query_proj,
    kv_down,
    kv_gain,
    kv_up,
    out_proj,
    ffn_gain,
    router_proj,
    shared_gate,
    shared_up,
    shared_down,
    expert_gate,
    expert_up,
    expert_down,
):
    me = lax.axis_index("tensor")
    place = lax.axis_index("dp")
    core = place % 2
    peers = lax.axis_size("tensor")
    dp_count = lax.axis_size("dp")
    nz = dp_count // 2
    local_rows = block_input.shape[0]
    rows = routes.shape[0]
    experts = expert_gate.shape[0]
    half = experts // 2
    capacity = rows * TOP * 9 // (8 * experts)
    qk_width = NOPE + ROPE
    query_scale = qk_width ** (-0.5)
    q_cols = query_proj.shape[1]
    heads = q_cols // qk_width
    d_rows = query_proj.shape[0]
    s_cols = shared_gate.shape[1]
    e_cols = expert_gate.shape[2]

    def in_order(array):
        return jnp.concatenate(
            [
                lax.dynamic_slice_in_dim(array, (me ^ k) * local_rows, local_rows, 0)
                for k in range(peers)
            ],
            axis=0,
        )

    small_rows = kv_down.shape[0]

    def column(vector):
        return jnp.pad(vector, (0, small_rows - vector.shape[0]))[:, None]

    small = jnp.concatenate(
        [kv_down, router_proj, column(attn_gain), column(ffn_gain), column(kv_gain)], axis=1
    )
    kv_cols = kv_down.shape[1]
    small_count = small.shape[1] + (-small.shape[1] % 16)
    small = jnp.pad(small, ((0, 0), (0, -small.shape[1] % 128)))
    small_blocks = gather_rows(small)
    x_blocks = gather_rows(block_input)
    go_blocks = gather_rows(out_grad)

    small_all = jnp.zeros((peers * small_rows, small.shape[1]), bf16)
    for k, block in enumerate(small_blocks):
        small_all = lax.dynamic_update_slice_in_dim(small_all, block, (me ^ k) * small_rows, 0)
    by_head = query_proj.reshape(d_rows, heads, qk_width)
    up_rows = kv_up.shape[0]
    chunks_up = kv_up.shape[1] // d_rows
    front_local = jnp.concatenate(
        [
            out_proj,
            by_head[:, :, :NOPE].reshape(d_rows, heads * NOPE).T,
            by_head[:, :, NOPE:].reshape(d_rows, heads * ROPE).T,
            small_all[:, :small_count].T,
            jnp.swapaxes(kv_up.reshape(up_rows, chunks_up, d_rows), 0, 1).reshape(-1, d_rows),
        ],
        axis=0,
    )
    at_q = heads * VD
    at_kv = at_q + q_cols
    at_router = at_kv + kv_cols
    at_gain = at_router + experts
    at_up = at_kv + small_count
    weight_front = lax.all_gather(front_local, "dp", axis=0)
    router_full = jnp.swapaxes(weight_front[:, at_router:at_gain, :], 0, 1).reshape(experts, D)
    gain_one = weight_front[:, at_gain, :].reshape(1, D).astype(f32)
    gain_two = weight_front[:, at_gain + 1, :].reshape(1, D).astype(f32)
    gain_latent = (
        weight_front[:, at_gain + 2, :]
        .reshape(-1, small_rows)[:, : kv_gain.shape[0]]
        .reshape(1, KVR)
        .astype(f32)
    )
    shared_local = jnp.concatenate([shared_gate.T, shared_up.T, shared_down], axis=0)
    shared_full = lax.all_gather(shared_local, "dp", axis=0)

    expert_local = jnp.concatenate(
        [jnp.swapaxes(expert_gate, 1, 2), jnp.swapaxes(expert_up, 1, 2), expert_down], axis=1
    )
    kept_part = lax.dynamic_slice_in_dim(expert_local, core * half, half, 0)
    sent_part = lax.dynamic_slice_in_dim(expert_local, (1 - core) * half, half, 0)
    got_part = swap_core(sent_part)
    first = core == 0
    pair_part = jnp.stack(
        [jnp.where(first, kept_part, got_part), jnp.where(first, got_part, kept_part)], axis=1
    ).reshape(half * 2 * 3 * e_cols, d_rows)
    size = 2 * 3 * e_cols
    pieces = [pair_part[s * size : (s + 1) * size] for s in range(half)]
    token_ids = jnp.arange(rows, dtype=jnp.int32)
    ranking = jnp.sum(
        jnp.where(drop_order[0][:, None] == token_ids[None, :], token_ids[:, None], 0), axis=0
    )
    expert_ids = jnp.arange(experts, dtype=jnp.int32)
    chosen = jnp.sum((routes[:, :, None] == expert_ids).astype(f32), axis=1)
    earlier = (ranking[None, :] < ranking[:, None]).astype(bf16)
    before = dot(earlier, chosen.astype(bf16)).astype(jnp.int32)
    slot_rank = jnp.sum(
        jnp.where(routes[:, :, None] == expert_ids, before[:, None, :], 0), axis=2
    )
    kept_mask = slot_rank < capacity
    flat_slot = in_order(jnp.where(kept_mask, routes * capacity + slot_rank, -1))
    routes_mine = in_order(routes)
    kept_mine = (flat_slot >= 0).astype(f32)
    slots = half * capacity
    slot_ids = jnp.arange(slots, dtype=jnp.int32)
    own_ids = core * slots + slot_ids
    far_ids = (1 - core) * slots + slot_ids

    def one_hot(ids):
        return (
            (flat_slot[:, 0:1] == ids[None, :]) | (flat_slot[:, 1:2] == ids[None, :])
        ).astype(bf16)

    own_hot = one_hot(own_ids)
    far_hot = one_hot(far_ids)

    def dispatch(values):
        return (
            dot_tn(own_hot, values, bf16).reshape(half, capacity, D),
            swap_core(dot_tn(far_hot, values, bf16)).reshape(half, capacity, D),
        )


    places = in_order(token_ids)
    half_width = ROPE // 2
    frequency = jnp.exp(
        -jnp.log(10000.0) * jnp.arange(half_width, dtype=jnp.int32).astype(f32) / half_width
    )
    angles = places.astype(f32)[:, None] * frequency[None, :]
    cosine, sine = jnp.cos(angles), jnp.sin(angles)
    cos_wide = jnp.tile(jnp.concatenate([cosine, cosine], axis=1), (1, heads))
    sin_wide = jnp.tile(jnp.concatenate([-sine, sine], axis=1), (1, heads))
    limit = jnp.maximum(places, prefixes[0] - 1)

    gathers = [Gather(p.reshape(2, 3 * e_cols, d_rows)) for p in pieces]
    flow = Flow()
    flow.add(gathers[0])
    (x_all,) = flow.tick(jnp.concatenate(x_blocks, axis=0))
    sizes = (heads, at_q, at_kv, at_gain, at_up, chunks_up, up_rows, query_scale)
    normed_all, q_nope, q_rope, compressed, latent, key_rope, key_value = front(
        x_all, weight_front, cos_wide, sin_wide, gain_latent, sizes
    )
    attended = [None] * peers
    out_parts = [None] * peers
    for k in list(range(peers - 1, -1, -1)):
        attended[k], part = attend(
            q_nope,
            q_rope,
            key_rope,
            key_value,
            places[None, :],
            limit[:, None],
            weight_front,
            k,
            local_rows,
            bf16 if k else f32,
        )
        out_parts[k] = send_back(part, k)

    go_all = jnp.concatenate([after(block, attended[0]) for block in go_blocks], axis=0)
    go_own, go_far = dispatch(go_all)
    x_here = block_input.astype(f32)
    own_part, go_own, go_far = sync([], out_parts[0], go_own, go_far)
    middle = x_here + own_part
    middle = middle + sum(part.astype(f32) for part in out_parts[1:])
    (middle,) = flow.tick(middle)
    normed_two = norm_rows(middle, gain_two).astype(bf16)
    if peers == 4:
        near = [send_back(normed_two, 1), send_back(normed_two, 2)]
        h2 = jnp.concatenate([normed_two, *near, *far_halves(near)], axis=0)
    else:
        h2 = jnp.concatenate(gather_rows(normed_two), axis=0)

    def blocks_of(array):
        return [array[k * local_rows : (k + 1) * local_rows] for k in range(peers)]

    flow.add(*gathers[1:2])
    (h2,) = flow.tick(h2)
    (ffn_part,), (h2_grad,), grad_shared, _ = ffn(
        [h2], [go_all], jnp.ones((1, rows), f32), shared_full, None, f32
    )
    grad_shared, h2 = flow.tick(grad_shared, h2)
    pair, h2 = sync([], pair_sums(grad_shared), h2)
    shared_chain = Chain(pair)
    flow.start(shared_chain)

    router = jax.nn.softmax(dot_nt(h2, router_full), axis=-1)
    route_gates = jnp.sum(
        jnp.where(routes_mine[:, :, None] == expert_ids, router[:, None, :], 0.0), axis=2
    )

    def slot_gates(ids):
        return jnp.sum(
            jnp.where(flat_slot[:, 0:1] == ids[None, :], route_gates[:, 0:1], 0.0)
            + jnp.where(flat_slot[:, 1:2] == ids[None, :], route_gates[:, 1:2], 0.0),
            axis=0,
        )

    gate_own = slot_gates(own_ids).reshape(half, capacity)
    gate_far = swap_core(slot_gates(far_ids).reshape(half, capacity))
    xe_own, xe_far = dispatch(h2)
    xe_own, gate_own = flow.tick(xe_own, gate_own)

    gate_grads, outs_own, outs_far, expert_sums = [], [], [], []

    def expert(s, weight, gate_own):
        gates = jnp.concatenate([gate_own[s : s + 1], gate_far[s : s + 1]], axis=1)
        outs, backs, grad, gate_grad = ffn(
            [xe_own, xe_far], [go_own, go_far], gates, weight, s, bf16
        )
        gate_grads.append(gate_grad)
        outs_own.append(outs[0])
        outs_far.append(outs[1])
        return backs[0], backs[1], grad

    def ids_of(s):
        base = jnp.arange(capacity, dtype=jnp.int32)[None, :] + s * capacity
        return [core * slots + base, (1 - core) * slots + base]

    weight_shape = (nz, 1, 2, 3 * e_cols, d_rows)
    weight_shape = (nz, 1, 2, 3 * e_cols, d_rows)
    weight_shape = (nz, 1, 2, 3 * e_cols, d_rows)
    def add_rows(total, s, here, there):
        (total,) = combine(total, flat_slot, ids_of(s), [here, swap_core(there)], local_rows, [f32])
        return total

    weight_shape = (nz, 1, 2, 3 * e_cols, d_rows)
    here, there, grad = expert(0, gathers[0].result().reshape(weight_shape), gate_own)
    for s in range(half - 1):
        flow.add(*gathers[s + 2 : s + 3])
        here, there, grad, gate_own = flow.tick(here, there, grad, gate_own)
        if s == 0:
            before = (here, there)
        weight = gathers[s + 1].result().reshape(weight_shape)
        here, there, next_grad = expert(s + 1, weight, gate_own)
        if s + 2 == half:
            here, there, next_grad = flow.tick(here, there, next_grad)
            break
        expert_sums.append(Chain(grad))
        flow.add(expert_sums[-1])
        here, there, h2_grad, grad = flow.tick(here, there, h2_grad, next_grad)
        if s == 0:
            h2_grad = add_rows(h2_grad, 0, *before)
        h2_grad = add_rows(h2_grad, s + 1, here, there)
        h2_grad, ffn_part = flow.tick(h2_grad, ffn_part)
        ffn_part = add_rows(ffn_part, s, outs_own[s], outs_far[s])
        h2_grad, ffn_part, gate_own = sync([], h2_grad, ffn_part, gate_own)
    if half == 2:
        h2_grad = add_rows(h2_grad, 0, *before)
    if half > 1:
        late_grads = [grad, next_grad]
    else:
        late_grads = [grad]
    h2_parts = combine(
        h2_grad,
        flat_slot,
        ids_of(half - 1),
        [here, swap_core(there)],
        local_rows,
        [f32] + [bf16] * (peers - 1),
    )
    h2_parts = [send_back(part, k) for k, part in enumerate(h2_parts)]
    late_grads, h2_parts[0] = sync([], late_grads, h2_parts[0])
    expert_sums += [sum_z(g) for g in late_grads]
    gate_grads = jnp.concatenate(gate_grads, axis=0)
    gate_grad_mine = gate_grads[:, :capacity].reshape(-1)
    gate_grad_here = swap_core(gate_grads[:, capacity:]).reshape(-1)
    gate_tokens = jnp.stack(
        [
            jnp.sum(
                jnp.where(flat_slot[:, k : k + 1] == own_ids[None, :], gate_grad_mine[None, :], 0.0)
                + jnp.where(
                    flat_slot[:, k : k + 1] == far_ids[None, :], gate_grad_here[None, :], 0.0
                ),
                axis=1,
            )
            for k in range(TOP)
        ],
        axis=1,
    )

    gates_here = sum_rows(blocks_of(gate_tokens))

    left = range(max(half - 2, 0), half)
    out_rows = [o for s in left for o in (outs_own[s], swap_core(outs_far[s]))]
    ffn_part, own_part, *out_rows = sync([], ffn_part, h2_parts[0], *out_rows)
    out_parts = combine(
        ffn_part,
        flat_slot,
        [i for s in left for i in ids_of(s)],
        out_rows,
        local_rows,
        [f32] + [bf16] * (peers - 1),
    )
    own_part, *out_parts = sync([], own_part, *out_parts)
    h2_grad_here = own_part + sum(part.astype(f32) for part in h2_parts[1:])

    router_here = router[:local_rows]
    route_grad = gates_here * kept_mine[:local_rows]
    router_grad = jnp.sum(
        jnp.where(
            routes_mine[:local_rows, :, None] == expert_ids, route_grad[:, :, None], 0.0
        ),
        axis=1,
    )
    logit_grad = (
        router_here * (router_grad - jnp.sum(router_here * router_grad, axis=-1, keepdims=True))
    ).astype(bf16)
    h2_grad_here = h2_grad_here + dot(logit_grad, router_full)
    middle_norm_grad, grad_gain_two = norm_back(middle, gain_two, h2_grad_here)
    middle_grad = out_grad.astype(f32) + middle_norm_grad
    own_rows = middle_grad.astype(bf16)
    if peers == 4:
        attn_grad = [own_rows, send_back(own_rows, 1), send_back(own_rows, 2), None]
    else:
        attn_grad = gather_rows(own_rows)

    h1_parts = [None] * peers
    query_grads = [None] * peers
    so_far = None
    finished = []
    for k in range(peers):
        query_grads[k], part, dkv, dkr = attend_back(
            attn_grad[k],
            q_nope,
            q_rope,
            key_rope,
            key_value,
            places[:, None],
            limit[None, :],
            cos_wide,
            sin_wide,
            weight_front,
            so_far,
            k,
            query_scale,
            bf16 if k else f32,
        )
        h1_parts[k] = send_back(part, k)
        if k == 0 and peers == 4:
            dkv, *near = sync([], dkv, *attn_grad[1:3])
            attn_grad[1:3] = near
            far = far_halves(near)
        if k == 2 and peers == 4:
            dkv, *far = sync([], dkv, *far)
            attn_grad[3] = jnp.concatenate(far, axis=0)
        if k > 1:
            dkv, h1_parts[k - 1] = sync([], dkv, h1_parts[k - 1])
        so_far = (dkv, dkr)

    query_grad = outer(query_grads, blocks_of(normed_all), d_rows)
    kv_grad, compressed_grad, grad_gain_latent = latent_back(
        dkv, dkr, compressed, cos_wide, sin_wide, gain_latent, weight_front, at_up, chunks_up, up_rows
    )
    query_grad, compressed_grad, kv_grad, h1_parts[-1] = sync(
        [], query_grad, compressed_grad, kv_grad, h1_parts[-1]
    )
    query_sum = sum_dp(query_grad)

    compressed_parts = [send_back(part, k) for k, part in enumerate(blocks_of(compressed_grad))]
    wide = KVR + 2 * ROPE
    small_grad = outer([compressed_grad], [normed_all], d_rows)
    small_grad, compressed_parts = sync([], small_grad, compressed_parts)
    gain_rows = jnp.stack(
        [
            grad_gain_two.reshape(dp_count, d_rows),
            jnp.pad(
                grad_gain_latent.reshape(dp_count, peers, kv_gain.shape[0]),
                ((0, 0), (0, 0), (0, small_rows - kv_gain.shape[0])),
            ).reshape(dp_count, d_rows),
        ],
        axis=1,
    )
    router_rows = jnp.swapaxes(dot_tn(logit_grad, normed_two).reshape(experts, dp_count, d_rows), 0, 1)
    extra_rows = jnp.concatenate([router_rows, gain_rows], axis=1).astype(bf16)
    extra_rows = jnp.pad(extra_rows, ((0, 0), (0, wide - kv_cols - extra_rows.shape[1]), (0, 0)))
    small_grad = jnp.concatenate([small_grad[:, :kv_cols], extra_rows], axis=1)
    share = wide // peers
    small_parts = [
        send_back(lax.dynamic_slice_in_dim(small_grad, (me ^ k) * share, share, 1), k)
        for k in range(peers)
    ]

    up_grad = outer([latent], [kv_grad], d_rows).reshape(chunks_up, dp_count, up_rows, d_rows)
    up_grad = jnp.swapaxes(up_grad, 0, 1).reshape(dp_count, chunks_up * up_rows, d_rows)
    out_grads = outer(attended, attn_grad, d_rows)
    out_grads, up_grad, small_parts = sync([], out_grads, up_grad, small_parts)
    small_mine = sum(part.astype(f32) for part in small_parts).astype(bf16)
    late_grad = jnp.concatenate([out_grads, up_grad, small_mine], axis=1)
    late_sum = sum_dp(late_grad)
    late_grad, out_parts, h1_parts[0] = sync([], late_grad, out_parts, h1_parts[0])
    out_parts = [send_back(part, k) for k, part in enumerate(out_parts)]

    compressed_round = sum(part.astype(f32) for part in compressed_parts).astype(bf16)[:, :kv_cols]
    down_full = jnp.swapaxes(weight_front[:, at_kv:at_router, :], 0, 1).reshape(kv_cols, D)
    h1_grad = h1_parts[0] + sum(part.astype(f32) for part in h1_parts[1:])
    h1_grad = h1_grad + dot(compressed_round, down_full)
    input_norm_grad, _ = norm_back(x_here, gain_one, h1_grad)
    input_grad = middle_grad + input_norm_grad
    output = (middle + sum(part.astype(f32) for part in out_parts)).astype(bf16)

    query_sum, late_sum = query_sum.astype(f32), late_sum.astype(f32)
    shared_sum = shared_chain.result()
    expert_sums = [
        e.result().astype(bf16) if isinstance(e, Chain) else e for e in expert_sums
    ]
    out_sum = late_sum[:at_q]
    query_chain_sum = query_sum
    nope_rows = heads * NOPE
    query_sum = jnp.concatenate(
        [
            query_sum[:nope_rows].reshape(heads, NOPE, d_rows),
            query_sum[nope_rows:].reshape(heads, ROPE, d_rows),
        ],
        axis=1,
    )
    query_sum = query_sum.reshape(q_cols, d_rows).T
    up_end = at_q + chunks_up * up_rows
    kvup_sum = jnp.swapaxes(
        late_sum[at_q:up_end].reshape(chunks_up, up_rows, d_rows), 0, 1
    ).reshape(up_rows, chunks_up * d_rows)

    small_sum = late_sum[up_end:]
    small_weight = jnp.pad(
        front_local[at_kv : at_kv + kv_cols].astype(f32), ((0, wide - kv_cols), (0, 0))
    )
    gain_part = jnp.sum(
        front_local[at_q:at_kv].astype(f32) * query_chain_sum, axis=0, keepdims=True
    ) + jnp.sum(
        lax.dynamic_slice_in_dim(small_weight, me * share, share, 0) * small_sum,
        axis=0,
        keepdims=True,
    )
    last = jnp.concatenate([small_sum, gain_part, jnp.zeros((7, d_rows), f32)], axis=0)
    by_peer = jnp.swapaxes(last.reshape(-1, peers, small_rows), 0, 1)
    last_parts = [
        send_back(lax.dynamic_index_in_dim(by_peer, me ^ k, 0, False), k) for k in range(peers)
    ]
    small_whole = jnp.zeros((wide, small_rows), f32)
    for k, part in enumerate(last_parts):
        small_whole = lax.dynamic_update_slice_in_dim(small_whole, part[:share], (me ^ k) * share, 0)
    gain_one_here = lax.dynamic_slice_in_dim(gain_one[0], (place * peers + me) * small_rows, small_rows)
    gain_one_out = sum(part[share] for part in last_parts) / gain_one_here
    kv_out = small_whole[:kv_cols].T
    router_out = small_whole[kv_cols : kv_cols + experts].T
    gain_two_out = small_whole[kv_cols + experts]
    gain_latent_out = small_whole[kv_cols + experts + 1, : kv_gain.shape[0]]

    mine = [lax.dynamic_index_in_dim(e, core, 0, False) for e in expert_sums]
    theirs = [swap_core(lax.dynamic_index_in_dim(e, 1 - core, 0, False)) for e in expert_sums]
    expert_grad = jnp.stack(
        [jnp.where(first, a, b) for a, b in zip(mine, theirs)]
        + [jnp.where(first, b, a) for a, b in zip(mine, theirs)],
        axis=0,
    ).astype(f32)

    return (
        output,
        input_grad,
        gain_one_out,
        query_sum,
        kv_out,
        gain_latent_out,
        kvup_sum,
        out_sum,
        gain_two_out,
        router_out,
        shared_sum[:s_cols].T,
        shared_sum[s_cols : 2 * s_cols].T,
        shared_sum[2 * s_cols :],
        jnp.swapaxes(expert_grad[:, :e_cols], 1, 2),
        jnp.swapaxes(expert_grad[:, e_cols : 2 * e_cols], 1, 2),
        expert_grad[:, 2 * e_cols :],
    )


def solution(mesh):
    placed = (
        P(("dp", "tensor"), None),
        P(("dp", "tensor"), None),
        P("dp", None),
        P("dp"),
        P("dp", None),
        P(("dp", "tensor")),
        P("dp", "tensor"),
        P(("dp", "tensor"), None),
        P(("dp", "tensor")),
        P("dp", "tensor"),
        P("tensor", "dp"),
        P(("dp", "tensor")),
        P(("dp", "tensor"), None),
        P("dp", "tensor"),
        P("dp", "tensor"),
        P("tensor", "dp"),
        P(None, "dp", "tensor"),
        P(None, "dp", "tensor"),
        P(None, "tensor", "dp"),
    )
    return jax.shard_map(
        on_device,
        mesh=mesh,
        in_specs=placed,
        out_specs=(
            P(("dp", "tensor"), None),
            P(("dp", "tensor"), None),
            P(("dp", "tensor")),
            P("dp", "tensor"),
            P(("dp", "tensor"), None),
            P(("dp", "tensor")),
            P("dp", "tensor"),
            P("tensor", "dp"),
            P(("dp", "tensor")),
            P(("dp", "tensor"), None),
            P("dp", "tensor"),
            P("dp", "tensor"),
            P("tensor", "dp"),
            P(None, "dp", "tensor"),
            P(None, "dp", "tensor"),
            P(None, "tensor", "dp"),
        ),
        check_vma=False,
    )
```
